32 devices in a mesh: groups: 2 (over y), ctx: 8 (over z, x), head: 2 (over core).
Axes of the slice: x: 2, y: 2, z: 4, core: 2. Of those that a mesh axis runs over, the one named last changes fastest.
Arguments:
- queries: bfloat16 [2048, 2048], P(('groups', 'ctx'), 'head'), parts along dimension 0, may hold values from -80 to 80
- keys: bfloat16 [2048, 512], P(('groups', 'ctx'), 'head'), parts along dimension 0, may hold values from -6 to 6
- values: bfloat16 [2048, 512], P(('groups', 'ctx'), 'head'), parts along dimension 0, may hold values from -6 to 6
- pattern: int32 [16, 8], P(('groups', 'ctx')), parts along dimension 0, may hold values from -1 to 7, as said below
- x_in: bfloat16 [2048, 1024], P(('groups', 'ctx'), 'head'), parts along dimension 0, may hold values from -2 to 2
- z_gate: bfloat16 [2048, 1024], P(('groups', 'ctx'), 'head'), parts along dimension 0, may hold values from -6 to 6
- bmat: bfloat16 [2048, 256], P(('groups', 'ctx'), 'head'), parts along dimension 0, may hold values from -6 to 6
- cmat: bfloat16 [2048, 256], P(('groups', 'ctx'), 'head'), parts along dimension 0, may hold values from -0.5 to 0.5
- log_decay: float32 [32, 1024], P(('groups', 'head'), 'ctx'), parts along dimension 0, may hold values from -2 to 0
- gain: float32 [1024], P('head'), may hold values from 0.1 to 1.9
Outputs:
- attn_out: bfloat16 [2048, 2048], P(('groups', 'ctx'), 'head'), parts along dimension 0
- ssm_out: bfloat16 [2048, 1024], P(('groups', 'ctx'), 'head'), parts along dimension 0
The draws below stay inside these ranges and needn't reach their ends.
There are 2 independent parts, one for each index of `groups`. The reference program is written for one: setup_inputs(seed, part) draws one part's arguments, and reference() takes and returns one part's arrays. A program takes and returns all parts, laid end to end along the dimension named above; an argument that names none is the same for every part. Nothing has to cross between parts.
Inputs may be any that keep to these rules, and one draw needn't show every extreme that they name: `pattern`: entry 0 of row q is q; the other entries are distinct blocks from q - 3 to q - 1, or -1 where no block is listed.
All inputs are finite; a program needn't handle non-finite values.
Results may differ from the reference program's by a relative error of at most 0.009.
Values may be sent and summed in bfloat16 or wider, within the bound.
A program may use at most 128 MiB of HBM per device.

```python
import jax
import jax.numpy as jnp
from jax import lax

BLK = 128
SCAN_BLK = 128
HD = 128
KVH = 4
QPK = 4
P_SIZE = 64
N = 128
HG = 8
SG = 2
KSEL = 8
MH = 16
TOKENS = 1024
NB = 8
WIN = 3


def head_speeds(key):
    inner = jax.random.fold_in(key, 7)
    pick_key, level_key = jax.random.split(inner)
    slow_share = 0.5
    slow_heads = jax.random.uniform(pick_key, (MH,)) < slow_share
    level = jax.random.uniform(level_key, (MH,))
    slow_rate = 0.3 * 2.0 ** level / TOKENS
    quick_speed = 2.4 ** level / 60.0
    return jnp.where(slow_heads, slow_rate, quick_speed)


def key_field(key):
    inner = jax.random.fold_in(key, 31)
    field = jnp.clip(jax.random.normal(inner, (NB, BLK, KVH * HD)), -6.0, 6.0)
    return field


def draw_keys(key, part):
    return key_field(key).reshape(TOKENS, KVH * HD).astype(jnp.bfloat16)


def draw_queries(key, part):
    inner = jax.random.fold_in(key, 37)
    field = jnp.clip(jax.random.normal(inner, (NB, BLK, KVH, QPK, HD)), -6.0, 6.0)
    return field.reshape(TOKENS, KVH * QPK * HD).astype(jnp.bfloat16)


def draw_pattern(key, part):
    span_size = max(WIN, KSEL - 1)
    raw_scores = jax.random.randint(key, (NB, span_size), 0, 1 << 20)
    distinct = raw_scores * span_size + jnp.arange(span_size, dtype=jnp.int32)[None, :]
    order = jnp.argsort(distinct, axis=1)
    offsets = order[:, :KSEL - 1].astype(jnp.int32) + 1
    block_ids = jnp.arange(NB, dtype=jnp.int32)
    picks = block_ids[:, None] - offsets
    picks = jnp.where((offsets <= WIN) & (picks >= 0), picks, -1)
    return jnp.concatenate([block_ids[:, None], picks], axis=1).astype(jnp.int32)


def draw_log_decay(key, part):
    reference_speed = head_speeds(key)
    inner = jax.random.fold_in(key, 9)
    rough_key, place_key, loss_key = jax.random.split(inner, 3)
    rough_approximation = jnp.exp(jax.random.uniform(rough_key, (MH, TOKENS), minval=-0.7, maxval=0.7))
    placement_sequence = jax.random.randint(place_key, (2,), 0, TOKENS)
    objective_numbers = jax.random.uniform(loss_key, (MH, 2), minval=0.2, maxval=0.5)
    offset_indices = jnp.arange(TOKENS)
    spike_occurrences = jnp.where(offset_indices[None, :] == placement_sequence[0], jnp.log1p(-objective_numbers[:, 0:1]), 0.0)
    spike_occurrences = spike_occurrences + jnp.where(offset_indices[None, :] == placement_sequence[1], jnp.log1p(-objective_numbers[:, 1:2]), 0.0)
    return (-reference_speed[:, None] * rough_approximation + spike_occurrences).astype(jnp.float32)


def draw_x_in(key, part):
    reference_speed = head_speeds(key)
    inner = jax.random.fold_in(key, 13)
    noise = jnp.clip(jax.random.normal(inner, (TOKENS, MH, P_SIZE)), -6.0, 6.0)
    scaled = noise * jnp.sqrt(2.0 * reference_speed)[None, :, None]
    return scaled.reshape(TOKENS, MH * P_SIZE).astype(jnp.bfloat16)


def shard_levels(stream_key, dims, cuts, low, high):
    level = 1.0
    for axis_at, blocks in cuts:
        steps = jax.random.uniform(jax.random.fold_in(jax.random.fold_in(stream_key, 6), axis_at), (blocks,), jnp.float32, low / len(cuts), high / len(cuts))
        level = level * jnp.repeat(jnp.exp(steps), dims[axis_at] // blocks).reshape((-1,) + (1,) * (len(dims) - 1 - axis_at))
    return level


def centred(stream_key, dims, scale, reach, cuts=(), held_as=jnp.bfloat16):
    entries = scale * jax.random.normal(stream_key, dims, jnp.float32)
    if cuts:
        entries = entries * shard_levels(stream_key, dims, cuts, -0.22, 0.18)
    return jnp.clip(entries, -reach, reach).astype(held_as)


def setup_inputs(seed: int = 0, part: int = 0) -> dict:
    seeds = jax.random.split(jax.random.key(seed), 11)
    own_keys = jax.random.split(jax.random.fold_in(seeds[10], part), 11)
    queries = draw_queries(jax.random.fold_in(jax.random.fold_in(seeds[10], part), 71), part)
    keys = draw_keys(jax.random.fold_in(jax.random.fold_in(seeds[10], part), 71), part)
    values = centred(own_keys[2], (TOKENS, KVH * HD), 1.0, 6.0, ((0, 8), (1, 2)))
    pattern = draw_pattern(jax.random.fold_in(jax.random.fold_in(seeds[10], part), 71), part)
    x_in = draw_x_in(jax.random.fold_in(jax.random.fold_in(seeds[10], part), 71), part)
    z_gate = centred(own_keys[5], (TOKENS, MH * P_SIZE), 1.0, 6.0, ((0, 8), (1, 2)))
    bmat = centred(own_keys[6], (TOKENS, SG * N), 1.0, 6.0, ((0, 8), (1, 2)))
    cmat = centred(own_keys[7], (TOKENS, SG * N), N ** -0.5, 0.5, ((0, 8), (1, 2)))
    log_decay = draw_log_decay(jax.random.fold_in(jax.random.fold_in(seeds[10], part), 71), part)
    gain = jnp.clip(1.0 + 0.18 * jax.random.normal(seeds[9], (MH * P_SIZE,), jnp.float32), 0.1, 1.9)
    return {"queries": queries, "keys": keys, "values": values, "pattern": pattern, "x_in": x_in, "z_gate": z_gate, "bmat": bmat, "cmat": cmat, "log_decay": log_decay, "gain": gain}


def ssd_block(state_in, inputs):
    x_vals, b_vals, c_vals, log_rates = inputs
    cumulative = jnp.cumsum(log_rates, axis=-1)
    length = cumulative.shape[-1]
    spread = cumulative[..., :, None] - cumulative[..., None, :]
    lower_tri = jnp.tril(jnp.ones((length, length), dtype=bool))
    decays = jnp.exp(jnp.where(lower_tri, spread, -jnp.inf))
    affinity = jnp.einsum('lgn,mgn->glm', c_vals, b_vals, precision=lax.Precision.HIGHEST)
    inside = jnp.einsum('glm,ghlm,mghp->lghp', affinity, decays, x_vals, precision=lax.Precision.HIGHEST)
    carried = jnp.einsum('lgn,ghpn->lghp', c_vals, state_in, precision=lax.Precision.HIGHEST)
    carried = carried * jnp.transpose(jnp.exp(cumulative), (2, 0, 1))[..., None]
    weights = jnp.exp(cumulative[..., -1:] - cumulative)
    summary = jnp.einsum('ghl,lghp,lgn->ghpn', weights, x_vals, b_vals, precision=lax.Precision.HIGHEST)
    state_out = jnp.exp(cumulative[..., -1])[..., None, None] * state_in + summary
    return (state_out, inside + carried)

def gate_scaled_rmsnorm(mixed_rows, z_gate, gain):
    gated_rows = mixed_rows * jax.nn.silu(z_gate.astype(jnp.float32))
    row_count = gated_rows.shape[0]
    grouped = gated_rows.reshape(row_count, -1, HG * P_SIZE)
    inverse_rms = lax.rsqrt(lax.optimization_barrier(jnp.mean(grouped * grouped, axis=-1, keepdims=True)) + 1e-05)
    scaled = grouped * inverse_rms * gain.reshape(-1, HG * P_SIZE)
    return scaled.reshape(row_count, -1).astype(jnp.bfloat16)

def attention(queries, keys, values, pattern):
    q_blocks = queries.astype(jnp.float32).reshape(NB, BLK, KVH, QPK, HD)
    k_blocks = keys.astype(jnp.float32).reshape(NB, BLK, KVH, HD)
    v_blocks = values.astype(jnp.float32).reshape(NB, BLK, KVH, HD)

    def one_block(inputs):
        q_rows, listed, block_no = inputs
        clipped = jnp.clip(listed, 0, NB - 1)
        key_sel = k_blocks[clipped].reshape(KSEL * BLK, KVH, HD)
        value_sel = v_blocks[clipped].reshape(KSEL * BLK, KVH, HD)
        scores = jnp.einsum('qkgd,mkd->kgqm', q_rows, key_sel) * HD ** (-0.5)
        key_pos = (listed[:, None] * BLK + jnp.arange(BLK, dtype=jnp.int32)[None, :]).reshape(-1)
        query_pos = block_no * BLK + jnp.arange(BLK, dtype=jnp.int32)
        usable = jnp.repeat(listed >= 0, BLK)
        allowed = usable[None, :] & (key_pos[None, :] <= query_pos[:, None])
        scores = jnp.where(allowed, scores, -jnp.inf)
        row_max = lax.optimization_barrier(jnp.max(scores, axis=-1, keepdims=True))
        expo = jnp.exp(scores - row_max)
        row_total = lax.optimization_barrier(jnp.sum(expo, axis=-1))
        rounded = lax.optimization_barrier(expo.astype(jnp.bfloat16)).astype(jnp.float32)
        mixed_rows = jnp.einsum('kgqm,mkd->qkgd', rounded, value_sel)
        mixed_rows = mixed_rows / jnp.transpose(row_total, (2, 0, 1))[..., None]
        return mixed_rows.reshape(BLK, KVH * QPK * HD)
    result = lax.map(one_block, (q_blocks, pattern, jnp.arange(NB, dtype=jnp.int32)))
    return result.reshape(TOKENS, KVH * QPK * HD).astype(jnp.bfloat16)

def reference(queries, keys, values, pattern, x_in, z_gate, bmat, cmat, log_decay, gain):
    block_count = TOKENS // SCAN_BLK
    x_vals = x_in.astype(jnp.float32).reshape(block_count, SCAN_BLK, SG, HG, P_SIZE)
    b_vals = bmat.astype(jnp.float32).reshape(block_count, SCAN_BLK, SG, N)
    c_vals = cmat.astype(jnp.float32).reshape(block_count, SCAN_BLK, SG, N)
    log_rates = jnp.transpose(log_decay.reshape(SG, HG, block_count, SCAN_BLK), (2, 0, 1, 3))
    zero_state = jnp.zeros((SG, HG, P_SIZE, N), jnp.float32)
    last_state, outputs = lax.scan(ssd_block, zero_state, (x_vals, b_vals, c_vals, log_rates))
    mixed_rows = outputs.reshape(TOKENS, MH * P_SIZE)
    ssm_out = gate_scaled_rmsnorm(mixed_rows, z_gate, gain)
    attn_out = attention(queries, keys, values, pattern)
    return (attn_out, ssm_out)
```

```python
import functools

import jax
import jax.numpy as jnp
from jax import lax
from jax.experimental import pallas as pl
from jax.experimental.pallas import tpu as pltpu
from jax.sharding import PartitionSpec as P

BLK = 128
HD = 128
P_SIZE = 64
N = 128
UNLISTED = -1e30
EXACT = lax.Precision.HIGHEST
MESH = pl.DeviceIdType.MESH


def dot(a, b, precision=None):
    return jnp.dot(a, b, preferred_element_type=jnp.float32, precision=precision)


def dot_rows(a, b):
    return lax.dot_general(a, b, (((1,), (1,)), ((), ())), preferred_element_type=jnp.float32)


def dot_state(c, state):
    if state.dtype == jnp.bfloat16:
        return dot(c, state)
    upper = state.astype(jnp.bfloat16)
    lower = (state - upper.astype(jnp.float32)).astype(jnp.bfloat16)
    return dot(c, upper) + dot(c, lower)


def kernel(
    n, state_type,
    q_ref, k_ref, v_ref, pat_ref, x_ref, z_ref, b_ref, c_ref, ld_ref, gain_ref,
    attn_ref, ssm_ref,
    kv_own, kv_in, ld_in, s_own, s_in, p_out, p_in, y_ref, grow_ref, acc_ref, max_ref, sum_ref,
    kv_send, kv_recv, ld_send, ld_recv, s_send, s_recv, p_send, p_recv,
):
    me = lax.axis_index("ctx")
    pair = me // 2
    side = me % 2
    partner = me + 1 - 2 * side
    has_next = me + 2 < n
    has_before = me >= 2
    heads = ld_ref.shape[0]
    width = heads * P_SIZE
    chunks = width // 128
    kv_heads = k_ref.shape[1] // HD
    members = q_ref.shape[1] // k_ref.shape[1]

    barrier = pltpu.get_barrier_semaphore()
    for away in (-2, -1, 1, 2):
        @pl.when((me + away >= 0) & (me + away < n))
        def _():
            pl.semaphore_signal(barrier, inc=1, device_id={"ctx": me + away}, device_id_type=MESH)

    def copy(src, dst, send_sem, recv_sem, target):
        return pltpu.make_async_remote_copy(
            src_ref=src, dst_ref=dst, send_sem=send_sem, recv_sem=recv_sem,
            device_id={"ctx": target}, device_id_type=MESH,
        )

    def kv_copy(src, slot, which, target):
        return copy(src, kv_in.at[slot], kv_send.at[which], kv_recv.at[slot], target)

    to_next = kv_copy(kv_own, 1, 0, me + 2)
    to_pair = kv_copy(kv_own, 0, 1, me + 1)
    relay_up = kv_copy(kv_in.at[1], 2, 2, me + 1)
    relay_down = kv_copy(kv_in.at[1], 0, 3, me - 1)
    ld_copy = copy(ld_ref, ld_in, ld_send, ld_recv, partner)
    s_copies = [
        copy(s_own.at[k], s_in.at[k], s_send.at[k], s_recv.at[k], partner) for k in range(chunks)
    ]
    p_copies = [
        copy(p_out.at[k], p_in.at[k], p_send.at[k], p_recv.at[k], me + 2) for k in range(chunks)
    ]

    kv_own[0] = k_ref[...]
    kv_own[1] = v_ref[...]

    row = lax.broadcasted_iota(jnp.int32, (BLK, BLK), 0)
    col = lax.broadcasted_iota(jnp.int32, (BLK, BLK), 1)
    log_rates = ld_ref[...]
    cum_row = dot(log_rates, (row <= col).astype(jnp.float32), EXACT)
    cum_col = cum_row.T
    head_of = (
        lax.broadcasted_iota(jnp.int32, (heads, width), 1) // P_SIZE
        == lax.broadcasted_iota(jnp.int32, (heads, width), 0)
    ).astype(jnp.float32)
    cum_wide = dot(cum_col, head_of, EXACT)
    total_own = cum_wide[BLK - 1 :, :]
    weighted = (x_ref[...].astype(jnp.float32) * jnp.exp(total_own - cum_wide)).astype(jnp.bfloat16)
    b_turned = b_ref[...].astype(jnp.float32).T.astype(jnp.bfloat16)
    summary = dot(b_turned, weighted).astype(state_type)
    for k in range(chunks):
        s_own[k] = summary[:, k * 128 : (k + 1) * 128]

    @pl.when(pair == 0)
    def _():
        p_in[...] = jnp.zeros_like(p_in)

    peers = jnp.minimum(me, 2) + jnp.minimum(n - 1 - me, 2)
    pl.semaphore_wait(barrier, peers)

    ld_copy.start()
    for each in s_copies:
        each.start()

    @pl.when(has_next)
    def _():
        to_next.start()

    @pl.when(side == 0)
    def _():
        to_pair.start()

    affinity = dot_rows(c_ref[...], b_ref[...])
    for k in range(chunks):
        x_pair = x_ref[:, k * 128 : (k + 1) * 128]
        halves = []
        for h in (2 * k, 2 * k + 1):
            spread = cum_col[:, h : h + 1] - cum_row[h : h + 1, :]
            decays = jnp.exp(jnp.where(row >= col, spread, -jnp.inf))
            halves.append(dot((affinity * decays).astype(jnp.bfloat16), x_pair))
        y_ref[:, k * 128 : (k + 1) * 128] = jnp.where(col < P_SIZE, halves[0], halves[1])
    grow_ref[...] = jnp.exp(cum_wide)

    def head_rows(c):
        return jnp.concatenate(
            [q_ref[:, (c * members + j) * HD : (c * members + j + 1) * HD] for j in range(members)],
            axis=0,
        )

    def scores_of(keys, c):
        return dot_rows(keys, head_rows(c)) * HD ** (-0.5)

    def own_block():
        key_at = lax.broadcasted_iota(jnp.int32, (BLK, members * BLK), 0)
        query_at = lax.broadcasted_iota(jnp.int32, (BLK, members * BLK), 1) % BLK
        for c in range(kv_heads):
            scores = scores_of(k_ref[:, c * HD : (c + 1) * HD], c)
            scores = jnp.where(key_at <= query_at, scores, UNLISTED)
            top = jnp.max(scores, axis=0, keepdims=True)
            expo = jnp.exp(scores - top)
            v_turned = v_ref[:, c * HD : (c + 1) * HD].astype(jnp.float32).T.astype(jnp.bfloat16)
            acc_ref[c] = dot(v_turned, expo.astype(jnp.bfloat16))
            max_ref[c] = top
            sum_ref[c] = jnp.sum(expo, axis=0, keepdims=True)

    def earlier_block(slot):
        listed = jnp.max(
            jnp.where(pat_ref[...] == me - 1 - slot, 0.0, UNLISTED), axis=1, keepdims=True
        )
        for c in range(kv_heads):
            scores = scores_of(kv_in[slot, 0, :, c * HD : (c + 1) * HD], c) + listed
            before = max_ref[c]
            top = jnp.maximum(before, jnp.max(scores, axis=0, keepdims=True))
            scale = jnp.exp(before - top)
            expo = jnp.exp(scores - top)
            v_turned = (
                kv_in[slot, 1, :, c * HD : (c + 1) * HD].astype(jnp.float32).T.astype(jnp.bfloat16)
            )
            acc_ref[c] = acc_ref[c] * scale + dot(v_turned, expo.astype(jnp.bfloat16))
            max_ref[c] = top
            sum_ref[c] = sum_ref[c] * scale + jnp.sum(expo, axis=0, keepdims=True)

    def arrive_and_use(slot):
        if slot != 1:
            kv_copy(kv_own, slot, 0, me).wait_recv()
        earlier_block(slot)

    ld_copy.wait_recv()
    total_other = dot(
        jnp.sum(ld_in[...], axis=1, keepdims=True).T, head_of, EXACT
    )
    decay_other = jnp.exp(total_other)
    decay_late = jnp.exp(jnp.where(side == 0, total_other, total_own))
    decay_pair = jnp.exp(total_other + total_own)
    for k in range(chunks):
        at = slice(k * 128, (k + 1) * 128)
        s_copies[k].wait_recv()

        @pl.when(pair == 0)
        def _():
            own, other = s_own[k].astype(jnp.float32), s_in[k].astype(jnp.float32)
            early, late = jnp.where(side == 0, own, other), jnp.where(side == 0, other, own)
            p_out[k] = (decay_late[:, at] * early + late).astype(state_type)

            @pl.when(has_next)
            def _():
                p_copies[k].start()

    @pl.when(has_before)
    def _():
        to_next.wait_recv()

        @pl.when(side == 0)
        def _():
            relay_up.start()

        @pl.when(side == 1)
        def _():
            relay_down.start()

            @pl.when(has_next)
            def _():
                relay_up.start()

    @pl.when(pair >= 1)
    def _():
        own_block()

    @pl.when(pair >= 2)
    def _():
        earlier_block(1)

    @pl.when(pair >= 3)
    def _():
        arrive_and_use(0)
        arrive_and_use(2)

    @pl.when(pair >= 1)
    def _():
        for k in range(chunks):
            at = slice(k * 128, (k + 1) * 128)
            p_copies[k].wait_recv()

            @pl.when(has_next)
            def _():
                own, other = s_own[k].astype(jnp.float32), s_in[k].astype(jnp.float32)
                early, late = jnp.where(side == 0, own, other), jnp.where(side == 0, other, own)
                joined = decay_late[:, at] * early + late
                p_out[k] = (decay_pair[:, at] * p_in[k].astype(jnp.float32) + joined).astype(
                    state_type
                )
                p_copies[k].start()

    c_rows = c_ref[...]
    square = jnp.zeros((BLK, 1), jnp.float32)
    for k in range(chunks):
        at = slice(k * 128, (k + 1) * 128)
        far = dot_state(c_rows, p_in[k])
        near = dot_state(c_rows, s_in[k])
        carried = jnp.where(side == 0, far, decay_other[:, at] * far + near)
        gate = z_ref[:, at].astype(jnp.float32)
        gated = (y_ref[:, at] + carried * grow_ref[:, at]) * (gate / (1.0 + jnp.exp(-gate)))
        y_ref[:, at] = gated
        square = square + jnp.sum(gated * gated, axis=1, keepdims=True)
    inverse = lax.rsqrt(square / width + 1e-05)
    ssm_ref[...] = (y_ref[...] * inverse * gain_ref[...]).astype(jnp.bfloat16)

    @pl.when(pair == 0)
    def _():
        own_block()

    @pl.when(pair == 1)
    def _():
        earlier_block(1)

    @pl.when((pair < 3) & (me >= 1))
    def _():
        arrive_and_use(0)

    @pl.when((pair < 3) & (me >= 3))
    def _():
        arrive_and_use(2)

    for c in range(kv_heads):
        mixed = acc_ref[c] / sum_ref[c]
        for j in range(members):
            head = c * members + j
            attn_ref[:, head * HD : (head + 1) * HD] = (
                mixed[:, j * BLK : (j + 1) * BLK].T.astype(jnp.bfloat16)
            )

    ld_copy.wait_send()
    for each in s_copies:
        each.wait_send()

    @pl.when(has_next)
    def _():
        to_next.wait_send()
        for each in p_copies:
            each.wait_send()

    @pl.when(side == 0)
    def _():
        to_pair.wait_send()

    @pl.when(has_before & ((side == 0) | has_next))
    def _():
        relay_up.wait_send()

    @pl.when(has_before & (side == 1))
    def _():
        relay_down.wait_send()


def on_device(n, queries, keys, values, pattern, x_in, z_gate, bmat, cmat, log_decay, gain):
    state_type = jnp.bfloat16 if n <= 16 else jnp.float32
    heads = log_decay.shape[0]
    width = heads * P_SIZE
    chunks = width // 128
    kv_heads = keys.shape[1] // HD
    rows = queries.shape[1] // keys.shape[1] * BLK
    states = pltpu.VMEM((chunks, N, 128), state_type)
    dma = pltpu.SemaphoreType.DMA
    return pl.pallas_call(
        functools.partial(kernel, n, state_type),
        out_shape=(
            jax.ShapeDtypeStruct(queries.shape, jnp.bfloat16),
            jax.ShapeDtypeStruct(x_in.shape, jnp.bfloat16),
        ),
        in_specs=[pl.BlockSpec(memory_space=pltpu.VMEM)] * 10,
        out_specs=(pl.BlockSpec(memory_space=pltpu.VMEM),) * 2,
        scratch_shapes=[
            pltpu.VMEM((2, BLK, keys.shape[1]), jnp.bfloat16),
            pltpu.VMEM((3, 2, BLK, keys.shape[1]), jnp.bfloat16),
            pltpu.VMEM(log_decay.shape, jnp.float32),
            states, states, states, states,
            pltpu.VMEM((BLK, width), jnp.float32),
            pltpu.VMEM((BLK, width), jnp.float32),
            pltpu.VMEM((kv_heads, HD, rows), jnp.float32),
            pltpu.VMEM((kv_heads, 1, rows), jnp.float32),
            pltpu.VMEM((kv_heads, 1, rows), jnp.float32),
            dma((4,)), dma((3,)), dma, dma,
            dma((chunks,)), dma((chunks,)), dma((chunks,)), dma((chunks,)),
        ],
        compiler_params=pltpu.CompilerParams(
            collective_id=0, has_side_effects=True, vmem_limit_bytes=32 * 1024 * 1024
        ),
    )(
        queries, keys, values, pattern, x_in, z_gate, bmat, cmat, log_decay,
        gain.reshape(1, -1),
    )


def solution(mesh):
    rows = P(("groups", "ctx"), "head")
    placed = (
        rows, rows, rows, P(("groups", "ctx"), None), rows, rows, rows, rows,
        P(("groups", "head"), "ctx"), P("head"),
    )
    return jax.shard_map(
        functools.partial(on_device, mesh.shape["ctx"]),
        mesh=mesh,
        in_specs=placed,
        out_specs=(rows, rows),
        check_vma=False,
    )
```

```python
import functools

import jax
import jax.numpy as jnp
from jax import lax
from jax.experimental import pallas as pl
from jax.experimental.pallas import tpu as pltpu
from jax.sharding import PartitionSpec as P

BLK = 128
HD = 128
P_SIZE = 64
N = 128
UNLISTED = -1e30
EXACT = lax.Precision.HIGHEST
MESH = pl.DeviceIdType.MESH


def dot(a, b, precision=None):
    return jnp.dot(a, b, preferred_element_type=jnp.float32, precision=precision)


def dot_rows(a, b):
    return lax.dot_general(a, b, (((1,), (1,)), ((), ())), preferred_element_type=jnp.float32)


def dot_state(c, state):
    if state.dtype == jnp.bfloat16:
        return dot(c, state)
    upper = state.astype(jnp.bfloat16)
    lower = (state - upper.astype(jnp.float32)).astype(jnp.bfloat16)
    return dot(c, upper) + dot(c, lower)


def kernel(
    n, state_type,
    q_hbm, k_hbm, v_hbm, pat_hbm, x_hbm, z_hbm, b_hbm, c_hbm, ld_hbm, gain_hbm,
    acc_ref, sum_ref, ssm_ref,
    q_ref, pat_ref, x_ref, z_ref, b_ref, c_ref, ld_ref, gain_ref,
    kv_own, kv_in, ld_in, s_own, s_in, p_out, p_in, y_ref, grow_ref, max_ref,
    load_sem, kv_send, kv_recv, ld_send, ld_recv, s_send, s_recv, p_send, p_recv,
):
    me = lax.axis_index("ctx")
    pair = me // 2
    side = me % 2
    partner = me + 1 - 2 * side
    has_next = me + 2 < n
    has_before = me >= 2
    heads = ld_ref.shape[0]
    width = heads * P_SIZE
    chunks = width // 128
    kv_heads = kv_own.shape[2] // HD
    members = q_ref.shape[1] // kv_own.shape[2]

    barrier = pltpu.get_barrier_semaphore()
    for away in (-2, -1, 1, 2):
        @pl.when((me + away >= 0) & (me + away < n))
        def _():
            pl.semaphore_signal(barrier, inc=1, device_id={"ctx": me + away}, device_id_type=MESH)

    moves = (
        (ld_hbm, ld_ref), (b_hbm, b_ref), (x_hbm, x_ref), (k_hbm, kv_own.at[0]),
        (v_hbm, kv_own.at[1]), (c_hbm, c_ref), (z_hbm, z_ref), (q_hbm, q_ref),
        (gain_hbm, gain_ref), (pat_hbm, pat_ref),
    )
    loads = [pltpu.make_async_copy(src, dst, load_sem.at[i]) for i, (src, dst) in enumerate(moves)]
    for each in loads:
        each.start()
    ld_load, b_load, x_load, k_load, v_load, c_load, z_load, q_load, gain_load, pat_load = loads

    def copy(src, dst, send_sem, recv_sem, target):
        return pltpu.make_async_remote_copy(
            src_ref=src, dst_ref=dst, send_sem=send_sem, recv_sem=recv_sem,
            device_id={"ctx": target}, device_id_type=MESH,
        )

    def kv_copy(src, slot, which, target):
        return copy(src, kv_in.at[slot], kv_send.at[which], kv_recv.at[slot], target)

    to_next = kv_copy(kv_own, 1, 0, me + 2)
    to_pair = kv_copy(kv_own, 0, 1, me + 1)
    relay_up = kv_copy(kv_in.at[1], 2, 2, me + 1)
    relay_down = kv_copy(kv_in.at[1], 0, 3, me - 1)
    ld_copy = copy(ld_ref, ld_in, ld_send, ld_recv, partner)
    s_copies = [
        copy(s_own.at[k], s_in.at[k], s_send.at[k], s_recv.at[k], partner) for k in range(chunks)
    ]
    p_copies = [
        copy(p_out.at[k], p_in.at[k], p_send.at[k], p_recv.at[k], me + 2) for k in range(chunks)
    ]

    @pl.when(pair == 0)
    def _():
        p_in[...] = jnp.zeros_like(p_in)

    row = lax.broadcasted_iota(jnp.int32, (BLK, BLK), 0)
    col = lax.broadcasted_iota(jnp.int32, (BLK, BLK), 1)
    head_of = (
        lax.broadcasted_iota(jnp.int32, (heads, width), 1) // P_SIZE
        == lax.broadcasted_iota(jnp.int32, (heads, width), 0)
    ).astype(jnp.float32)

    def per_head_pair(k, matrix_of):
        x_pair = x_ref[:, k * 128 : (k + 1) * 128]
        first = dot(matrix_of(2 * k).astype(jnp.bfloat16), x_pair)
        second = dot(matrix_of(2 * k + 1).astype(jnp.bfloat16), x_pair)
        return jnp.where(col < P_SIZE, first, second)

    ld_load.wait()
    cum_row = dot(ld_ref[...], (row <= col).astype(jnp.float32), EXACT)
    total = cum_row[:, BLK - 1 :]
    fading = jnp.exp(total - cum_row)
    b_load.wait()
    b_turned = b_ref[...].astype(jnp.float32).T
    x_load.wait()
    for k in range(chunks):
        summary = per_head_pair(k, lambda h: b_turned * fading[h : h + 1, :])
        s_own[k] = summary.astype(state_type)

    peers = jnp.minimum(me, 2) + jnp.minimum(n - 1 - me, 2)
    pl.semaphore_wait(barrier, peers)

    ld_copy.start()
    for each in s_copies:
        each.start()
    k_load.wait()
    v_load.wait()

    @pl.when(has_next)
    def _():
        to_next.start()

    cum_col = cum_row.T
    c_load.wait()
    affinity = dot_rows(c_ref[...], b_ref[...])
    grow = dot(jnp.exp(cum_col), head_of, EXACT)
    z_load.wait()
    for k in range(chunks):
        at = slice(k * 128, (k + 1) * 128)

        def mixing(h):
            spread = cum_col[:, h : h + 1] - cum_row[h : h + 1, :]
            return affinity * jnp.exp(jnp.where(row >= col, spread, -jnp.inf))

        z = z_ref[:, at].astype(jnp.float32)
        gate = z / (1.0 + jnp.exp(-z))
        y_ref[:, at] = per_head_pair(k, mixing) * gate
        grow_ref[:, at] = grow[:, at] * gate
    q_load.wait()
    pat_load.wait()
    gain_load.wait()

    def head_rows(c):
        return jnp.concatenate(
            [q_ref[:, (c * members + j) * HD : (c * members + j + 1) * HD] for j in range(members)],
            axis=0,
        )

    def scores_of(keys, c):
        return dot_rows(keys, head_rows(c)) * HD ** (-0.5)

    def own_block():
        key_at = lax.broadcasted_iota(jnp.int32, (BLK, members * BLK), 0)
        query_at = lax.broadcasted_iota(jnp.int32, (BLK, members * BLK), 1) % BLK
        for c in range(kv_heads):
            scores = scores_of(kv_own[0, :, c * HD : (c + 1) * HD], c)
            scores = jnp.where(key_at <= query_at, scores, UNLISTED)
            top = jnp.max(scores, axis=0, keepdims=True)
            expo = jnp.exp(scores - top)
            v_turned = kv_own[1, :, c * HD : (c + 1) * HD].astype(jnp.float32).T.astype(jnp.bfloat16)
            acc_ref[c] = dot(v_turned, expo.astype(jnp.bfloat16))
            max_ref[c] = top
            sum_ref[c] = jnp.sum(expo, axis=0, keepdims=True)

    def earlier_block(slot):
        listed = jnp.max(
            jnp.where(pat_ref[...] == me - 1 - slot, 0.0, UNLISTED), axis=1, keepdims=True
        )
        for c in range(kv_heads):
            scores = scores_of(kv_in[slot, 0, :, c * HD : (c + 1) * HD], c) + listed
            before = max_ref[c]
            top = jnp.maximum(before, jnp.max(scores, axis=0, keepdims=True))
            scale = jnp.exp(before - top)
            expo = jnp.exp(scores - top)
            v_turned = (
                kv_in[slot, 1, :, c * HD : (c + 1) * HD].astype(jnp.float32).T.astype(jnp.bfloat16)
            )
            acc_ref[c] = acc_ref[c] * scale + dot(v_turned, expo.astype(jnp.bfloat16))
            max_ref[c] = top
            sum_ref[c] = sum_ref[c] * scale + jnp.sum(expo, axis=0, keepdims=True)

    def arrive_and_use(slot):
        if slot != 1:
            kv_copy(kv_own, slot, 0, me).wait_recv()
        earlier_block(slot)

    ld_copy.wait_recv()
    wide_own = dot(total.T, head_of, EXACT)
    wide_other = dot(jnp.sum(ld_in[...], axis=1, keepdims=True).T, head_of, EXACT)
    decay_other = jnp.exp(wide_other)
    decay_late = jnp.exp(jnp.where(side == 0, wide_other, wide_own))
    decay_pair = jnp.exp(wide_other + wide_own)

    def joined(k):
        own, other = s_own[k].astype(jnp.float32), s_in[k].astype(jnp.float32)
        early, late = jnp.where(side == 0, own, other), jnp.where(side == 0, other, own)
        return decay_late[:, k * 128 : (k + 1) * 128] * early + late

    for k in range(chunks):
        s_copies[k].wait_recv()

        @pl.when((pair == 0) & has_next)
        def _():
            p_out[k] = joined(k).astype(state_type)
            p_copies[k].start()

    @pl.when(side == 0)
    def _():
        to_pair.start()

    @pl.when(has_before)
    def _():
        to_next.wait_recv()

        @pl.when(side == 0)
        def _():
            relay_up.start()

        @pl.when(side == 1)
        def _():
            relay_down.start()

            @pl.when(has_next)
            def _():
                relay_up.start()

    @pl.when(side == 1)
    def _():
        for k in range(chunks):
            at = slice(k * 128, (k + 1) * 128)
            growth = grow_ref[:, at]
            y_ref[:, at] = y_ref[:, at] + dot_state(c_ref[...], s_in[k]) * growth
            grow_ref[:, at] = growth * decay_other[:, at]

    @pl.when(pair >= 1)
    def _():
        own_block()

    @pl.when(pair >= 2)
    def _():
        earlier_block(1)

    @pl.when(pair >= 3)
    def _():
        arrive_and_use(0)
        arrive_and_use(2)

    for k in range(chunks):
        at = slice(k * 128, (k + 1) * 128)

        @pl.when(pair >= 1)
        def _():
            p_copies[k].wait_recv()

            @pl.when(has_next)
            def _():
                p_out[k] = (
                    decay_pair[:, at] * p_in[k].astype(jnp.float32) + joined(k)
                ).astype(state_type)
                p_copies[k].start()

        y_ref[:, at] = y_ref[:, at] + dot_state(c_ref[...], p_in[k]) * grow_ref[:, at]
    gated = y_ref[...]
    square = jnp.sum(gated * gated, axis=1, keepdims=True)
    inverse = lax.rsqrt(square / width + 1e-05)
    ssm_ref[...] = (gated * inverse * gain_ref[...]).astype(jnp.bfloat16)

    @pl.when(pair == 0)
    def _():
        own_block()

    @pl.when(pair == 1)
    def _():
        earlier_block(1)

    @pl.when((pair < 3) & (me >= 1))
    def _():
        arrive_and_use(0)

    @pl.when((pair < 3) & (me >= 3))
    def _():
        arrive_and_use(2)

    ld_copy.wait_send()
    for each in s_copies:
        each.wait_send()

    @pl.when(has_next)
    def _():
        to_next.wait_send()
        for each in p_copies:
            each.wait_send()

    @pl.when(side == 0)
    def _():
        to_pair.wait_send()

    @pl.when(has_before & ((side == 0) | has_next))
    def _():
        relay_up.wait_send()

    @pl.when(has_before & (side == 1))
    def _():
        relay_down.wait_send()


def finish(acc_ref, sum_ref, ssm_ref, attn_hbm, ssm_hbm, attn_ref, sems):
    kv_heads, _, rows = acc_ref.shape
    ssm_copy = pltpu.make_async_copy(ssm_ref, ssm_hbm, sems.at[kv_heads])
    ssm_copy.start()
    copies = []
    for c in range(kv_heads):
        mixed = acc_ref[c] / sum_ref[c]
        for j in range(rows // BLK):
            head = c * (rows // BLK) + j
            attn_ref[:, head * HD : (head + 1) * HD] = (
                mixed[:, j * BLK : (j + 1) * BLK].T.astype(jnp.bfloat16)
            )
        at = pl.ds(c * rows, rows)
        copies.append(
            pltpu.make_async_copy(attn_ref.at[:, at], attn_hbm.at[:, at], sems.at[c])
        )
        copies[-1].start()
    for each in copies:
        each.wait()
    ssm_copy.wait()


def on_device(n, queries, keys, values, pattern, x_in, z_gate, bmat, cmat, log_decay, gain):
    state_type = jnp.bfloat16 if n <= 16 else jnp.float32
    heads = log_decay.shape[0]
    width = heads * P_SIZE
    chunks = width // 128
    kv_heads = keys.shape[1] // HD
    rows = queries.shape[1] // keys.shape[1] * BLK
    states = pltpu.VMEM((chunks, N, 128), state_type)
    dma = pltpu.SemaphoreType.DMA
    in_hbm = pl.BlockSpec(memory_space=pltpu.HBM)
    in_vmem = pl.BlockSpec(memory_space=pltpu.VMEM)

    def held(array):
        return pltpu.VMEM(array.shape, array.dtype)

    gain = gain.reshape(1, -1)
    far_inputs = [
        pltpu.with_memory_space_constraint(each, pltpu.HBM)
        for each in (queries, keys, values, pattern, x_in, z_gate, bmat, cmat, log_decay, gain)
    ]
    unscaled, totals, ssm = pl.pallas_call(
        functools.partial(kernel, n, state_type),
        out_shape=(
            jax.ShapeDtypeStruct((kv_heads, HD, rows), jnp.float32),
            jax.ShapeDtypeStruct((kv_heads, 1, rows), jnp.float32),
            jax.ShapeDtypeStruct(x_in.shape, jnp.bfloat16),
        ),
        in_specs=[in_hbm] * 10,
        out_specs=(in_vmem,) * 3,
        scratch_shapes=[
            held(queries), held(pattern), held(x_in), held(z_gate), held(bmat), held(cmat),
            held(log_decay), held(gain),
            pltpu.VMEM((2, BLK, keys.shape[1]), jnp.bfloat16),
            pltpu.VMEM((3, 2, BLK, keys.shape[1]), jnp.bfloat16),
            pltpu.VMEM(log_decay.shape, jnp.float32),
            states, states, states, states,
            pltpu.VMEM((BLK, width), jnp.float32),
            pltpu.VMEM((BLK, width), jnp.float32),
            pltpu.VMEM((kv_heads, 1, rows), jnp.float32),
            dma((10,)), dma((4,)), dma((3,)), dma, dma,
            dma((chunks,)), dma((chunks,)), dma((chunks,)), dma((chunks,)),
        ],
        compiler_params=pltpu.CompilerParams(
            collective_id=0, has_side_effects=True, vmem_limit_bytes=32 * 1024 * 1024
        ),
    )(*far_inputs)
    return pl.pallas_call(
        finish,
        out_shape=(
            jax.ShapeDtypeStruct(queries.shape, jnp.bfloat16),
            jax.ShapeDtypeStruct(x_in.shape, jnp.bfloat16),
        ),
        in_specs=[in_vmem] * 3,
        out_specs=(in_hbm, in_hbm),
        scratch_shapes=[held(queries), dma((kv_heads + 1,))],
        compiler_params=pltpu.CompilerParams(vmem_limit_bytes=32 * 1024 * 1024),
    )(unscaled, totals, ssm)


def solution(mesh):
    rows = P(("groups", "ctx"), "head")
    placed = (
        rows, rows, rows, P(("groups", "ctx"), None), rows, rows, rows, rows,
        P(("groups", "head"), "ctx"), P("head"),
    )
    return jax.shard_map(
        functools.partial(on_device, mesh.shape["ctx"]),
        mesh=mesh,
        in_specs=placed,
        out_specs=(rows, rows),
        check_vma=False,
    )
```

```python
import functools

import jax
import jax.numpy as jnp
from jax import lax
from jax.experimental import pallas as pl
from jax.experimental.pallas import tpu as pltpu
from jax.sharding import PartitionSpec as P

BLK = 128
HD = 128
P_SIZE = 64
N = 128
UNLISTED = -1e30
EXACT = lax.Precision.HIGHEST
MESH = pl.DeviceIdType.MESH


def dot(a, b, precision=None):
    return jnp.dot(a, b, preferred_element_type=jnp.float32, precision=precision)


def dot_rows(a, b):
    return lax.dot_general(a, b, (((1,), (1,)), ((), ())), preferred_element_type=jnp.float32)


def dot_state(c, state):
    if state.dtype == jnp.bfloat16:
        return dot(c, state)
    upper = state.astype(jnp.bfloat16)
    lower = (state - upper.astype(jnp.float32)).astype(jnp.bfloat16)
    return dot(c, upper) + dot(c, lower)


def kernel(
    n, state_type,
    q_hbm, k_hbm, v_hbm, pat_hbm, x_hbm, z_hbm, b_hbm, c_hbm, ld_hbm, gain_hbm,
    acc_ref, sum_ref, ssm_ref,
    q_ref, pat_ref, x_ref, z_ref, b_ref, c_ref, ld_ref, gain_ref,
    kv_own, kv_in, ld_in, s_own, s_in, p_out, p_in, joint_ref, y_ref, grow_ref, max_ref,
    load_sem, kv_send, kv_recv, ld_send, ld_recv, s_send, s_recv, p_send, p_recv,
):
    me = lax.axis_index("ctx")
    pair = me // 2
    side = me % 2
    partner = me + 1 - 2 * side
    has_next = me + 2 < n
    has_before = me >= 2
    heads = ld_ref.shape[0]
    width = heads * P_SIZE
    chunks = width // 128
    kv_heads = kv_own.shape[2] // HD
    members = q_ref.shape[1] // kv_own.shape[2]

    barrier = pltpu.get_barrier_semaphore()
    pl.semaphore_signal(barrier, inc=1, device_id={"ctx": partner}, device_id_type=MESH)
    for away in (-2, 2):
        @pl.when((me + away >= 0) & (me + away < n))
        def _():
            pl.semaphore_signal(barrier, inc=1, device_id={"ctx": me + away}, device_id_type=MESH)

    moves = (
        (k_hbm, kv_own.at[0]), (v_hbm, kv_own.at[1]), (ld_hbm, ld_ref), (b_hbm, b_ref),
        (x_hbm, x_ref), (c_hbm, c_ref), (z_hbm, z_ref), (q_hbm, q_ref),
        (gain_hbm, gain_ref), (pat_hbm, pat_ref),
    )
    loads = [pltpu.make_async_copy(src, dst, load_sem.at[i]) for i, (src, dst) in enumerate(moves)]
    for each in loads:
        each.start()
    k_load, v_load, ld_load, b_load, x_load, c_load, z_load, q_load, gain_load, pat_load = loads

    def copy(src, dst, send_sem, recv_sem, target):
        return pltpu.make_async_remote_copy(
            src_ref=src, dst_ref=dst, send_sem=send_sem, recv_sem=recv_sem,
            device_id={"ctx": target}, device_id_type=MESH,
        )

    def kv_copies(src, slot, which, target):
        return [
            copy(
                src.at[half], kv_in.at[slot, half], kv_send.at[which, half],
                kv_recv.at[slot, half], target,
            )
            for half in (0, 1)
        ]

    to_next = kv_copies(kv_own, 1, 0, me + 2)
    to_pair = kv_copies(kv_own, 0, 1, partner)
    relay_down = kv_copies(kv_in.at[1], 0, 2, partner)
    forward = kv_copies(kv_in.at[0], 2, 3, me + 2)
    forwards = has_next & (me >= 1)
    ld_copy = copy(ld_ref, ld_in, ld_send, ld_recv, partner)
    s_copies = [
        copy(s_own.at[k], s_in.at[k], s_send.at[k], s_recv.at[k], partner) for k in range(chunks)
    ]
    p_copies = [
        copy(p_out.at[k], p_in.at[k], p_send.at[k], p_recv.at[k], me + 2) for k in range(chunks)
    ]

    @pl.when(pair == 0)
    def _():
        p_in[...] = jnp.zeros_like(p_in)

    row = lax.broadcasted_iota(jnp.int32, (BLK, BLK), 0)
    col = lax.broadcasted_iota(jnp.int32, (BLK, BLK), 1)
    head_of = (
        lax.broadcasted_iota(jnp.int32, (heads, width), 1) // P_SIZE
        == lax.broadcasted_iota(jnp.int32, (heads, width), 0)
    ).astype(jnp.float32)

    def per_head_pair(k, matrix_of):
        x_pair = x_ref[:, k * 128 : (k + 1) * 128]
        first = dot(matrix_of(2 * k).astype(jnp.bfloat16), x_pair)
        second = dot(matrix_of(2 * k + 1).astype(jnp.bfloat16), x_pair)
        return jnp.where(col < P_SIZE, first, second)

    ld_load.wait()
    cum_row = dot(ld_ref[...], (row <= col).astype(jnp.float32), EXACT)
    total = cum_row[:, BLK - 1 :]
    fading = jnp.exp(total - cum_row)
    b_load.wait()
    b_turned = b_ref[...].astype(jnp.float32).T

    peers = 1 + has_before.astype(jnp.int32) + has_next.astype(jnp.int32)
    pl.semaphore_wait(barrier, peers)
    k_load.wait()
    v_load.wait()

    @pl.when(has_next)
    def _():
        for each in to_next:
            each.start()

    ld_copy.start()
    x_load.wait()
    for k in range(chunks):
        summary = per_head_pair(k, lambda h: b_turned * fading[h : h + 1, :])
        s_own[k] = summary.astype(state_type)
        s_copies[k].start()

    @pl.when(side == 0)
    def _():
        for each in to_pair:
            each.start()

    cum_col = cum_row.T
    c_load.wait()
    affinity = dot_rows(c_ref[...], b_ref[...])
    grow = dot(jnp.exp(cum_col), head_of, EXACT)
    z_load.wait()
    for k in range(chunks):
        at = slice(k * 128, (k + 1) * 128)

        def mixing(h):
            spread = cum_col[:, h : h + 1] - cum_row[h : h + 1, :]
            return affinity * jnp.exp(jnp.where(row >= col, spread, -jnp.inf))

        z = z_ref[:, at].astype(jnp.float32)
        gate = z / (1.0 + jnp.exp(-z))
        y_ref[:, at] = per_head_pair(k, mixing) * gate
        grow_ref[:, at] = grow[:, at] * gate
    q_load.wait()
    pat_load.wait()
    gain_load.wait()

    def head_rows(c):
        return jnp.concatenate(
            [q_ref[:, (c * members + j) * HD : (c * members + j + 1) * HD] for j in range(members)],
            axis=0,
        )

    def scores_of(keys, c):
        return dot_rows(keys, head_rows(c)) * HD ** (-0.5)

    def own_block():
        key_at = lax.broadcasted_iota(jnp.int32, (BLK, members * BLK), 0)
        query_at = lax.broadcasted_iota(jnp.int32, (BLK, members * BLK), 1) % BLK
        for c in range(kv_heads):
            scores = scores_of(kv_own[0, :, c * HD : (c + 1) * HD], c)
            scores = jnp.where(key_at <= query_at, scores, UNLISTED)
            top = jnp.max(scores, axis=0, keepdims=True)
            expo = jnp.exp(scores - top)
            v_turned = kv_own[1, :, c * HD : (c + 1) * HD].astype(jnp.float32).T.astype(jnp.bfloat16)
            acc_ref[c] = dot(v_turned, expo.astype(jnp.bfloat16))
            max_ref[c] = top
            sum_ref[c] = jnp.sum(expo, axis=0, keepdims=True)

    def earlier_block(slot):
        listed = jnp.max(
            jnp.where(pat_ref[...] == me - 1 - slot, 0.0, UNLISTED), axis=1, keepdims=True
        )
        for c in range(kv_heads):
            scores = scores_of(kv_in[slot, 0, :, c * HD : (c + 1) * HD], c) + listed
            before = max_ref[c]
            top = jnp.maximum(before, jnp.max(scores, axis=0, keepdims=True))
            scale = jnp.exp(before - top)
            expo = jnp.exp(scores - top)
            v_turned = (
                kv_in[slot, 1, :, c * HD : (c + 1) * HD].astype(jnp.float32).T.astype(jnp.bfloat16)
            )
            acc_ref[c] = acc_ref[c] * scale + dot(v_turned, expo.astype(jnp.bfloat16))
            max_ref[c] = top
            sum_ref[c] = sum_ref[c] * scale + jnp.sum(expo, axis=0, keepdims=True)

    ld_copy.wait_recv()
    wide_own = dot(total.T, head_of, EXACT)
    wide_other = dot(jnp.sum(ld_in[...], axis=1, keepdims=True).T, head_of, EXACT)
    decay_other = jnp.exp(wide_other)
    decay_late = jnp.exp(jnp.where(side == 0, wide_other, wide_own))
    decay_pair = jnp.exp(wide_other + wide_own)

    def joined(k):
        own, other = s_own[k].astype(jnp.float32), s_in[k].astype(jnp.float32)
        early, late = jnp.where(side == 0, own, other), jnp.where(side == 0, other, own)
        return decay_late[:, k * 128 : (k + 1) * 128] * early + late

    for k in range(chunks):
        s_copies[k].wait_recv()
        joint = joined(k)

        @pl.when((pair == 0) & has_next)
        def _():
            p_out[k] = joint.astype(state_type)
            p_copies[k].start()

        @pl.when((pair >= 1) & has_next)
        def _():
            joint_ref[k] = joint

    @pl.when(has_before)
    def _():
        for half in (0, 1):
            to_next[half].wait_recv()

            @pl.when(side == 1)
            def _():
                relay_down[half].start()

    @pl.when(side == 1)
    def _():
        for k in range(chunks):
            at = slice(k * 128, (k + 1) * 128)
            growth = grow_ref[:, at]
            y_ref[:, at] = y_ref[:, at] + dot_state(c_ref[...], s_in[k]) * growth
            grow_ref[:, at] = growth * decay_other[:, at]

    def pass_on(half):
        to_pair[half].wait_recv()

        @pl.when(forwards)
        def _():
            forward[half].start()

    @pl.when(pair >= 2)
    def _():
        own_block()
        earlier_block(1)
        pass_on(0)

    @pl.when(pair >= 3)
    def _():
        pass_on(1)
        earlier_block(0)

    for k in range(chunks):
        at = slice(k * 128, (k + 1) * 128)

        @pl.when(pair >= 1)
        def _():
            p_copies[k].wait_recv()

            @pl.when(has_next)
            def _():
                p_out[k] = (
                    decay_pair[:, at] * p_in[k].astype(jnp.float32) + joint_ref[k]
                ).astype(state_type)
                p_copies[k].start()

        if k == min(1, chunks - 1):
            @pl.when(pair == 2)
            def _():
                pass_on(1)

        y_ref[:, at] = y_ref[:, at] + dot_state(c_ref[...], p_in[k]) * grow_ref[:, at]

    @pl.when(pair < 2)
    def _():
        own_block()

        @pl.when(me >= 1)
        def _():
            pass_on(0)
            pass_on(1)

    gated = y_ref[...]
    square = jnp.sum(gated * gated, axis=1, keepdims=True)
    inverse = lax.rsqrt(square / width + 1e-05)
    ssm_ref[...] = (gated * inverse * gain_ref[...]).astype(jnp.bfloat16)

    @pl.when(pair == 1)
    def _():
        earlier_block(1)

    @pl.when((pair < 3) & (me >= 1))
    def _():
        earlier_block(0)

    @pl.when(me >= 3)
    def _():
        for each in forward:
            each.wait_recv()
        earlier_block(2)

    ld_copy.wait_send()
    for each in s_copies:
        each.wait_send()

    @pl.when(has_next)
    def _():
        for each in to_next + p_copies:
            each.wait_send()

    @pl.when(side == 0)
    def _():
        for each in to_pair:
            each.wait_send()

    @pl.when(has_before & (side == 1))
    def _():
        for each in relay_down:
            each.wait_send()

    @pl.when(forwards)
    def _():
        for each in forward:
            each.wait_send()


def finish(acc_ref, sum_ref, ssm_ref, attn_hbm, ssm_hbm, attn_ref, sems):
    kv_heads, _, rows = acc_ref.shape
    ssm_copy = pltpu.make_async_copy(ssm_ref, ssm_hbm, sems.at[kv_heads])
    ssm_copy.start()
    copies = []
    for c in range(kv_heads):
        mixed = acc_ref[c] / sum_ref[c]
        for j in range(rows // BLK):
            head = c * (rows // BLK) + j
            attn_ref[:, head * HD : (head + 1) * HD] = (
                mixed[:, j * BLK : (j + 1) * BLK].T.astype(jnp.bfloat16)
            )
        at = pl.ds(c * rows, rows)
        copies.append(
            pltpu.make_async_copy(attn_ref.at[:, at], attn_hbm.at[:, at], sems.at[c])
        )
        copies[-1].start()
    for each in copies:
        each.wait()
    ssm_copy.wait()


def on_device(n, queries, keys, values, pattern, x_in, z_gate, bmat, cmat, log_decay, gain):
    state_type = jnp.bfloat16 if n <= 16 else jnp.float32
    heads = log_decay.shape[0]
    width = heads * P_SIZE
    chunks = width // 128
    kv_heads = keys.shape[1] // HD
    rows = queries.shape[1] // keys.shape[1] * BLK
    states = pltpu.VMEM((chunks, N, 128), state_type)
    dma = pltpu.SemaphoreType.DMA
    in_hbm = pl.BlockSpec(memory_space=pltpu.HBM)
    in_vmem = pl.BlockSpec(memory_space=pltpu.VMEM)

    def held(array):
        return pltpu.VMEM(array.shape, array.dtype)

    gain = gain.reshape(1, -1)
    far_inputs = [
        pltpu.with_memory_space_constraint(each, pltpu.HBM)
        for each in (queries, keys, values, pattern, x_in, z_gate, bmat, cmat, log_decay, gain)
    ]
    unscaled, totals, ssm = pl.pallas_call(
        functools.partial(kernel, n, state_type),
        out_shape=(
            jax.ShapeDtypeStruct((kv_heads, HD, rows), jnp.float32),
            jax.ShapeDtypeStruct((kv_heads, 1, rows), jnp.float32),
            jax.ShapeDtypeStruct(x_in.shape, jnp.bfloat16),
        ),
        in_specs=[in_hbm] * 10,
        out_specs=(in_vmem,) * 3,
        scratch_shapes=[
            held(queries), held(pattern), held(x_in), held(z_gate), held(bmat), held(cmat),
            held(log_decay), held(gain),
            pltpu.VMEM((2, BLK, keys.shape[1]), jnp.bfloat16),
            pltpu.VMEM((3, 2, BLK, keys.shape[1]), jnp.bfloat16),
            pltpu.VMEM(log_decay.shape, jnp.float32),
            states, states, states, states,
            pltpu.VMEM((chunks, N, 128), jnp.float32),
            pltpu.VMEM((BLK, width), jnp.float32),
            pltpu.VMEM((BLK, width), jnp.float32),
            pltpu.VMEM((kv_heads, 1, rows), jnp.float32),
            dma((10,)), dma((4, 2)), dma((3, 2)), dma, dma,
            dma((chunks,)), dma((chunks,)), dma((chunks,)), dma((chunks,)),
        ],
        compiler_params=pltpu.CompilerParams(
            collective_id=0, has_side_effects=True, vmem_limit_bytes=32 * 1024 * 1024
        ),
    )(*far_inputs)
    return pl.pallas_call(
        finish,
        out_shape=(
            jax.ShapeDtypeStruct(queries.shape, jnp.bfloat16),
            jax.ShapeDtypeStruct(x_in.shape, jnp.bfloat16),
        ),
        in_specs=[in_vmem] * 3,
        out_specs=(in_hbm, in_hbm),
        scratch_shapes=[held(queries), dma((kv_heads + 1,))],
        compiler_params=pltpu.CompilerParams(vmem_limit_bytes=32 * 1024 * 1024),
    )(unscaled, totals, ssm)


def solution(mesh):
    rows = P(("groups", "ctx"), "head")
    placed = (
        rows, rows, rows, P(("groups", "ctx"), None), rows, rows, rows, rows,
        P(("groups", "head"), "ctx"), P("head"),
    )
    return jax.shard_map(
        functools.partial(on_device, mesh.shape["ctx"]),
        mesh=mesh,
        in_specs=placed,
        out_specs=(rows, rows),
        check_vma=False,
    )
```

```python
import functools

import jax
import jax.numpy as jnp
from jax import lax
from jax.experimental import pallas as pl
from jax.experimental.pallas import tpu as pltpu
from jax.sharding import PartitionSpec as P

BLK = 128
HD = 128
P_SIZE = 64
N = 128
UNLISTED = -1e30
EXACT = lax.Precision.HIGHEST
MESH = pl.DeviceIdType.MESH


def dot(a, b, precision=None):
    return jnp.dot(a, b, preferred_element_type=jnp.float32, precision=precision)


def dot_rows(a, b):
    return lax.dot_general(a, b, (((1,), (1,)), ((), ())), preferred_element_type=jnp.float32)


def dot_state(c, state):
    if state.dtype == jnp.bfloat16:
        return dot(c, state)
    upper = state.astype(jnp.bfloat16)
    lower = (state - upper.astype(jnp.float32)).astype(jnp.bfloat16)
    return dot(c, upper) + dot(c, lower)


def kernel(
    n, state_type,
    q_hbm, k_hbm, v_hbm, pat_hbm, x_hbm, z_hbm, b_hbm, c_hbm, ld_hbm, gain_hbm,
    acc_ref, sum_ref, ssm_ref,
    q_ref, pat_ref, x_ref, z_ref, b_ref, c_ref, ld_ref, gain_ref,
    kv_own, kv_in, ld_in, s_own, s_in, p_out, p_in, joint_ref, y_ref, grow_ref, max_ref,
    load_sem, kv_send, kv_recv, ld_send, ld_recv, s_send, s_recv, p_send, p_recv,
):
    me = lax.axis_index("ctx")
    pair = me // 2
    side = me % 2
    partner = me + 1 - 2 * side
    has_next = me + 2 < n
    has_before = me >= 2
    heads = ld_ref.shape[0]
    width = heads * P_SIZE
    chunks = width // 128
    kv_heads = kv_own.shape[2] // HD
    members = q_ref.shape[1] // kv_own.shape[2]

    barrier = pltpu.get_barrier_semaphore()
    pl.semaphore_signal(barrier, inc=1, device_id={"ctx": partner}, device_id_type=MESH)
    for away in (-2, 2):
        @pl.when((me + away >= 0) & (me + away < n))
        def _():
            pl.semaphore_signal(barrier, inc=1, device_id={"ctx": me + away}, device_id_type=MESH)

    moves = (
        (k_hbm, kv_own.at[0]), (v_hbm, kv_own.at[1]), (ld_hbm, ld_ref), (b_hbm, b_ref),
        (x_hbm, x_ref), (c_hbm, c_ref), (z_hbm, z_ref), (q_hbm, q_ref),
        (gain_hbm, gain_ref), (pat_hbm, pat_ref),
    )
    loads = [pltpu.make_async_copy(src, dst, load_sem.at[i]) for i, (src, dst) in enumerate(moves)]
    for each in loads:
        each.start()
    k_load, v_load, ld_load, b_load, x_load, c_load, z_load, q_load, gain_load, pat_load = loads

    def copy(src, dst, send_sem, recv_sem, target):
        return pltpu.make_async_remote_copy(
            src_ref=src, dst_ref=dst, send_sem=send_sem, recv_sem=recv_sem,
            device_id={"ctx": target}, device_id_type=MESH,
        )

    def kv_copies(src, slot, which, target):
        return [
            copy(
                src.at[half], kv_in.at[slot, half], kv_send.at[which, half],
                kv_recv.at[slot, half], target,
            )
            for half in (0, 1)
        ]

    to_next = kv_copies(kv_own, 1, 0, me + 2)
    to_pair = kv_copies(kv_own, 0, 1, partner)
    relay_down = kv_copies(kv_in.at[1], 0, 2, partner)
    forward = kv_copies(kv_in.at[0], 2, 3, me + 2)
    forwards = has_next & (me >= 1)
    ld_copy = copy(ld_ref, ld_in, ld_send, ld_recv, partner)
    s_copies = [
        copy(s_own.at[k], s_in.at[k], s_send.at[k], s_recv.at[k], partner) for k in range(chunks)
    ]
    p_copies = [
        copy(p_out.at[k], p_in.at[k], p_send.at[k], p_recv.at[k], me + 2) for k in range(chunks)
    ]

    @pl.when(pair == 0)
    def _():
        p_in[...] = jnp.zeros_like(p_in)

    row = lax.broadcasted_iota(jnp.int32, (BLK, BLK), 0)
    col = lax.broadcasted_iota(jnp.int32, (BLK, BLK), 1)
    head_of = (
        lax.broadcasted_iota(jnp.int32, (heads, width), 1) // P_SIZE
        == lax.broadcasted_iota(jnp.int32, (heads, width), 0)
    ).astype(jnp.float32)

    def per_head_pair(k, matrix_of):
        x_pair = x_ref[:, k * 128 : (k + 1) * 128]
        first = dot(matrix_of(2 * k).astype(jnp.bfloat16), x_pair)
        second = dot(matrix_of(2 * k + 1).astype(jnp.bfloat16), x_pair)
        return jnp.where(col < P_SIZE, first, second)

    ld_load.wait()
    cum_row = dot(ld_ref[...], (row <= col).astype(jnp.float32), EXACT)
    total = cum_row[:, BLK - 1 :]
    fading = jnp.exp(total - cum_row)
    b_load.wait()
    b_turned = b_ref[...].astype(jnp.float32).T

    peers = 1 + has_before.astype(jnp.int32) + has_next.astype(jnp.int32)
    pl.semaphore_wait(barrier, peers)
    ld_copy.start()
    x_load.wait()
    for k in range(chunks):
        summary = per_head_pair(k, lambda h: b_turned * fading[h : h + 1, :])
        s_own[k] = summary.astype(state_type)
        s_copies[k].start()

    k_load.wait()
    v_load.wait()

    @pl.when(has_next)
    def _():
        for each in to_next:
            each.start()

    cum_col = cum_row.T
    c_load.wait()
    affinity = dot_rows(c_ref[...], b_ref[...])
    grow = dot(jnp.exp(cum_col), head_of, EXACT)
    z_load.wait()
    for k in range(chunks):
        at = slice(k * 128, (k + 1) * 128)

        def mixing(h):
            spread = cum_col[:, h : h + 1] - cum_row[h : h + 1, :]
            return affinity * jnp.exp(jnp.where(row >= col, spread, -jnp.inf))

        z = z_ref[:, at].astype(jnp.float32)
        gate = z / (1.0 + jnp.exp(-z))
        y_ref[:, at] = per_head_pair(k, mixing) * gate
        grow_ref[:, at] = grow[:, at] * gate
    q_load.wait()
    pat_load.wait()
    gain_load.wait()

    def head_rows(c):
        return jnp.concatenate(
            [q_ref[:, (c * members + j) * HD : (c * members + j + 1) * HD] for j in range(members)],
            axis=0,
        )

    def scores_of(keys, c):
        return dot_rows(keys, head_rows(c)) * HD ** (-0.5)

    def own_block():
        key_at = lax.broadcasted_iota(jnp.int32, (BLK, members * BLK), 0)
        query_at = lax.broadcasted_iota(jnp.int32, (BLK, members * BLK), 1) % BLK
        for c in range(kv_heads):
            scores = scores_of(kv_own[0, :, c * HD : (c + 1) * HD], c)
            scores = jnp.where(key_at <= query_at, scores, UNLISTED)
            top = jnp.max(scores, axis=0, keepdims=True)
            expo = jnp.exp(scores - top)
            v_turned = kv_own[1, :, c * HD : (c + 1) * HD].astype(jnp.float32).T.astype(jnp.bfloat16)
            acc_ref[c] = dot(v_turned, expo.astype(jnp.bfloat16))
            max_ref[c] = top
            sum_ref[c] = jnp.sum(expo, axis=0, keepdims=True)

    def earlier_block(slot):
        listed = jnp.max(
            jnp.where(pat_ref[...] == me - 1 - slot, 0.0, UNLISTED), axis=1, keepdims=True
        )
        for c in range(kv_heads):
            scores = scores_of(kv_in[slot, 0, :, c * HD : (c + 1) * HD], c) + listed
            before = max_ref[c]
            top = jnp.maximum(before, jnp.max(scores, axis=0, keepdims=True))
            scale = jnp.exp(before - top)
            expo = jnp.exp(scores - top)
            v_turned = (
                kv_in[slot, 1, :, c * HD : (c + 1) * HD].astype(jnp.float32).T.astype(jnp.bfloat16)
            )
            acc_ref[c] = acc_ref[c] * scale + dot(v_turned, expo.astype(jnp.bfloat16))
            max_ref[c] = top
            sum_ref[c] = sum_ref[c] * scale + jnp.sum(expo, axis=0, keepdims=True)

    ld_copy.wait_recv()
    wide_own = dot(total.T, head_of, EXACT)
    wide_other = dot(jnp.sum(ld_in[...], axis=1, keepdims=True).T, head_of, EXACT)
    decay_other = jnp.exp(wide_other)
    decay_late = jnp.exp(jnp.where(side == 0, wide_other, wide_own))
    decay_pair = jnp.exp(wide_other + wide_own)

    def joined(k):
        own, other = s_own[k].astype(jnp.float32), s_in[k].astype(jnp.float32)
        early, late = jnp.where(side == 0, own, other), jnp.where(side == 0, other, own)
        return decay_late[:, k * 128 : (k + 1) * 128] * early + late

    for k in range(chunks):
        s_copies[k].wait_recv()
        joint = joined(k)

        @pl.when((pair == 0) & has_next)
        def _():
            p_out[k] = joint.astype(state_type)
            p_copies[k].start()

        @pl.when((pair >= 1) & has_next)
        def _():
            joint_ref[k] = joint

    @pl.when(side == 0)
    def _():
        for each in to_pair:
            each.start()

    @pl.when(has_before)
    def _():
        for half in (0, 1):
            to_next[half].wait_recv()

            @pl.when(side == 1)
            def _():
                relay_down[half].start()

    @pl.when(side == 1)
    def _():
        for k in range(chunks):
            at = slice(k * 128, (k + 1) * 128)
            growth = grow_ref[:, at]
            y_ref[:, at] = y_ref[:, at] + dot_state(c_ref[...], s_in[k]) * growth
            grow_ref[:, at] = growth * decay_other[:, at]

    def pass_on(half):
        to_pair[half].wait_recv()

        @pl.when(forwards)
        def _():
            forward[half].start()

    @pl.when(pair >= 2)
    def _():
        own_block()
        earlier_block(1)

    @pl.when(pair >= 3)
    def _():
        pass_on(0)
        pass_on(1)
        earlier_block(0)

    for k in range(chunks):
        at = slice(k * 128, (k + 1) * 128)

        @pl.when(pair >= 1)
        def _():
            p_copies[k].wait_recv()

            @pl.when(has_next)
            def _():
                p_out[k] = (
                    decay_pair[:, at] * p_in[k].astype(jnp.float32) + joint_ref[k]
                ).astype(state_type)
                p_copies[k].start()

        y_ref[:, at] = y_ref[:, at] + dot_state(c_ref[...], p_in[k]) * grow_ref[:, at]

    @pl.when(pair < 2)
    def _():
        own_block()

    @pl.when((pair < 3) & (me >= 1))
    def _():
        pass_on(0)
        pass_on(1)

    gated = y_ref[...]
    square = jnp.sum(gated * gated, axis=1, keepdims=True)
    inverse = lax.rsqrt(square / width + 1e-05)
    ssm_ref[...] = (gated * inverse * gain_ref[...]).astype(jnp.bfloat16)

    @pl.when(pair == 1)
    def _():
        earlier_block(1)

    @pl.when((pair < 3) & (me >= 1))
    def _():
        earlier_block(0)

    @pl.when(me >= 3)
    def _():
        for each in forward:
            each.wait_recv()
        earlier_block(2)

    ld_copy.wait_send()
    for each in s_copies:
        each.wait_send()

    @pl.when(has_next)
    def _():
        for each in to_next + p_copies:
            each.wait_send()

    @pl.when(side == 0)
    def _():
        for each in to_pair:
            each.wait_send()

    @pl.when(has_before & (side == 1))
    def _():
        for each in relay_down:
            each.wait_send()

    @pl.when(forwards)
    def _():
        for each in forward:
            each.wait_send()


def finish(acc_ref, sum_ref, ssm_ref, attn_hbm, ssm_hbm, attn_ref, sems):
    kv_heads, _, rows = acc_ref.shape
    ssm_copy = pltpu.make_async_copy(ssm_ref, ssm_hbm, sems.at[kv_heads])
    ssm_copy.start()
    copies = []
    for c in range(kv_heads):
        mixed = acc_ref[c] / sum_ref[c]
        for j in range(rows // BLK):
            head = c * (rows // BLK) + j
            attn_ref[:, head * HD : (head + 1) * HD] = (
                mixed[:, j * BLK : (j + 1) * BLK].T.astype(jnp.bfloat16)
            )
        at = pl.ds(c * rows, rows)
        copies.append(
            pltpu.make_async_copy(attn_ref.at[:, at], attn_hbm.at[:, at], sems.at[c])
        )
        copies[-1].start()
    for each in copies:
        each.wait()
    ssm_copy.wait()


def on_device(n, queries, keys, values, pattern, x_in, z_gate, bmat, cmat, log_decay, gain):
    state_type = jnp.bfloat16 if n <= 16 else jnp.float32
    heads = log_decay.shape[0]
    width = heads * P_SIZE
    chunks = width // 128
    kv_heads = keys.shape[1] // HD
    rows = queries.shape[1] // keys.shape[1] * BLK
    states = pltpu.VMEM((chunks, N, 128), state_type)
    dma = pltpu.SemaphoreType.DMA
    in_hbm = pl.BlockSpec(memory_space=pltpu.HBM)
    in_vmem = pl.BlockSpec(memory_space=pltpu.VMEM)

    def held(array):
        return pltpu.VMEM(array.shape, array.dtype)

    gain = gain.reshape(1, -1)
    far_inputs = [
        pltpu.with_memory_space_constraint(each, pltpu.HBM)
        for each in (queries, keys, values, pattern, x_in, z_gate, bmat, cmat, log_decay, gain)
    ]
    unscaled, totals, ssm = pl.pallas_call(
        functools.partial(kernel, n, state_type),
        out_shape=(
            jax.ShapeDtypeStruct((kv_heads, HD, rows), jnp.float32),
            jax.ShapeDtypeStruct((kv_heads, 1, rows), jnp.float32),
            jax.ShapeDtypeStruct(x_in.shape, jnp.bfloat16),
        ),
        in_specs=[in_hbm] * 10,
        out_specs=(in_vmem,) * 3,
        scratch_shapes=[
            held(queries), held(pattern), held(x_in), held(z_gate), held(bmat), held(cmat),
            held(log_decay), held(gain),
            pltpu.VMEM((2, BLK, keys.shape[1]), jnp.bfloat16),
            pltpu.VMEM((3, 2, BLK, keys.shape[1]), jnp.bfloat16),
            pltpu.VMEM(log_decay.shape, jnp.float32),
            states, states, states, states,
            pltpu.VMEM((chunks, N, 128), jnp.float32),
            pltpu.VMEM((BLK, width), jnp.float32),
            pltpu.VMEM((BLK, width), jnp.float32),
            pltpu.VMEM((kv_heads, 1, rows), jnp.float32),
            dma((10,)), dma((4, 2)), dma((3, 2)), dma, dma,
            dma((chunks,)), dma((chunks,)), dma((chunks,)), dma((chunks,)),
        ],
        compiler_params=pltpu.CompilerParams(
            collective_id=0, has_side_effects=True, vmem_limit_bytes=32 * 1024 * 1024
        ),
    )(*far_inputs)
    return pl.pallas_call(
        finish,
        out_shape=(
            jax.ShapeDtypeStruct(queries.shape, jnp.bfloat16),
            jax.ShapeDtypeStruct(x_in.shape, jnp.bfloat16),
        ),
        in_specs=[in_vmem] * 3,
        out_specs=(in_hbm, in_hbm),
        scratch_shapes=[held(queries), dma((kv_heads + 1,))],
        compiler_params=pltpu.CompilerParams(vmem_limit_bytes=32 * 1024 * 1024),
    )(unscaled, totals, ssm)


def solution(mesh):
    rows = P(("groups", "ctx"), "head")
    placed = (
        rows, rows, rows, P(("groups", "ctx"), None), rows, rows, rows, rows,
        P(("groups", "head"), "ctx"), P("head"),
    )
    return jax.shard_map(
        functools.partial(on_device, mesh.shape["ctx"]),
        mesh=mesh,
        in_specs=placed,
        out_specs=(rows, rows),
        check_vma=False,
    )
```

```python
import functools

import jax
import jax.numpy as jnp
from jax import lax
from jax.experimental import pallas as pl
from jax.experimental.pallas import tpu as pltpu
from jax.sharding import PartitionSpec as P

BLK = 128
HD = 128
P_SIZE = 64
N = 128
UNLISTED = -1e30
EXACT = lax.Precision.HIGHEST
MESH = pl.DeviceIdType.MESH


def dot(a, b, precision=None):
    return jnp.dot(a, b, preferred_element_type=jnp.float32, precision=precision)


def dot_rows(a, b):
    return lax.dot_general(a, b, (((1,), (1,)), ((), ())), preferred_element_type=jnp.float32)


def dot_state(c, state):
    if state.dtype == jnp.bfloat16:
        return dot(c, state)
    upper = state.astype(jnp.bfloat16)
    lower = (state - upper.astype(jnp.float32)).astype(jnp.bfloat16)
    return dot(c, upper) + dot(c, lower)


def kernel(
    n, state_type,
    q_hbm, k_hbm, v_hbm, pat_hbm, x_hbm, z_hbm, b_hbm, c_hbm, ld_hbm, gain_hbm,
    acc_ref, sum_ref, ssm_ref,
    q_ref, pat_ref, x_ref, z_ref, b_ref, c_ref, ld_ref, gain_ref,
    kv_own, kv_in, ld_in, s_own, s_in, p_out, p_in, joint_ref, y_ref, grow_ref, max_ref,
    load_sem, kv_send, kv_recv, ld_send, ld_recv, s_send, s_recv, p_send, p_recv,
):
    me = lax.axis_index("ctx")
    pair = me // 2
    side = me % 2
    partner = me + 1 - 2 * side
    has_next = me + 2 < n
    has_before = me >= 2
    heads = ld_ref.shape[0]
    width = heads * P_SIZE
    chunks = width // 128
    kv_heads = kv_own.shape[2] // HD
    members = q_ref.shape[1] // kv_own.shape[2]

    barrier = pltpu.get_barrier_semaphore()
    pl.semaphore_signal(barrier, inc=1, device_id={"ctx": partner}, device_id_type=MESH)
    for away in (-2, 2):
        @pl.when((me + away >= 0) & (me + away < n))
        def _():
            pl.semaphore_signal(barrier, inc=1, device_id={"ctx": me + away}, device_id_type=MESH)

    moves = (
        (k_hbm, kv_own.at[0]), (v_hbm, kv_own.at[1]), (ld_hbm, ld_ref), (b_hbm, b_ref),
        (x_hbm, x_ref), (c_hbm, c_ref), (z_hbm, z_ref), (q_hbm, q_ref),
        (gain_hbm, gain_ref), (pat_hbm, pat_ref),
    )
    loads = [pltpu.make_async_copy(src, dst, load_sem.at[i]) for i, (src, dst) in enumerate(moves)]
    for each in loads:
        each.start()
    k_load, v_load, ld_load, b_load, x_load, c_load, z_load, q_load, gain_load, pat_load = loads

    def copy(src, dst, send_sem, recv_sem, target):
        return pltpu.make_async_remote_copy(
            src_ref=src, dst_ref=dst, send_sem=send_sem, recv_sem=recv_sem,
            device_id={"ctx": target}, device_id_type=MESH,
        )

    def kv_copies(src, slot, which, target):
        return [
            copy(
                src.at[half], kv_in.at[slot, half], kv_send.at[which, half],
                kv_recv.at[slot, half], target,
            )
            for half in (0, 1)
        ]

    to_next = kv_copies(kv_own, 1, 0, me + 2)
    to_pair = kv_copies(kv_own, 0, 1, partner)
    relay_down = kv_copies(kv_in.at[1], 0, 2, partner)
    forward = kv_copies(kv_in.at[0], 2, 3, me + 2)
    forwards = has_next & (me >= 1)
    ld_copy = copy(ld_ref, ld_in, ld_send, ld_recv, partner)
    s_copies = [
        copy(s_own.at[k], s_in.at[k], s_send.at[k], s_recv.at[k], partner) for k in range(chunks)
    ]
    p_copies = [
        copy(p_out.at[k], p_in.at[k], p_send.at[k], p_recv.at[k], me + 2) for k in range(chunks)
    ]

    @pl.when(pair == 0)
    def _():
        p_in[...] = jnp.zeros_like(p_in)

    row = lax.broadcasted_iota(jnp.int32, (BLK, BLK), 0)
    col = lax.broadcasted_iota(jnp.int32, (BLK, BLK), 1)
    head_of = (
        lax.broadcasted_iota(jnp.int32, (heads, width), 1) // P_SIZE
        == lax.broadcasted_iota(jnp.int32, (heads, width), 0)
    ).astype(jnp.float32)

    def per_head_pair(k, matrix_of):
        x_pair = x_ref[:, k * 128 : (k + 1) * 128]
        first = dot(matrix_of(2 * k).astype(jnp.bfloat16), x_pair)
        second = dot(matrix_of(2 * k + 1).astype(jnp.bfloat16), x_pair)
        return jnp.where(col < P_SIZE, first, second)

    ld_load.wait()
    cum_row = dot(ld_ref[...], (row <= col).astype(jnp.float32), EXACT)
    total = cum_row[:, BLK - 1 :]
    fading = jnp.exp(total - cum_row)
    b_load.wait()
    b_turned = b_ref[...].astype(jnp.float32).T
    x_load.wait()
    for k in range(chunks):
        summary = per_head_pair(k, lambda h: b_turned * fading[h : h + 1, :])
        s_own[k] = summary.astype(state_type)

    peers = 1 + has_before.astype(jnp.int32) + has_next.astype(jnp.int32)
    pl.semaphore_wait(barrier, peers)
    ld_copy.start()
    for each in s_copies:
        each.start()
    k_load.wait()
    v_load.wait()

    @pl.when(has_next)
    def _():
        for each in to_next:
            each.start()

    cum_col = cum_row.T
    c_load.wait()
    affinity = dot_rows(c_ref[...], b_ref[...])
    grow = dot(jnp.exp(cum_col), head_of, EXACT)
    z_load.wait()
    for k in range(chunks):
        at = slice(k * 128, (k + 1) * 128)

        def mixing(h):
            spread = cum_col[:, h : h + 1] - cum_row[h : h + 1, :]
            return affinity * jnp.exp(jnp.where(row >= col, spread, -jnp.inf))

        z = z_ref[:, at].astype(jnp.float32)
        gate = z / (1.0 + jnp.exp(-z))
        y_ref[:, at] = per_head_pair(k, mixing) * gate
        grow_ref[:, at] = grow[:, at] * gate
    q_load.wait()
    pat_load.wait()
    gain_load.wait()

    def head_rows(c):
        return jnp.concatenate(
            [q_ref[:, (c * members + j) * HD : (c * members + j + 1) * HD] for j in range(members)],
            axis=0,
        )

    def scores_of(keys, c):
        return dot_rows(keys, head_rows(c)) * HD ** (-0.5)

    def own_block():
        key_at = lax.broadcasted_iota(jnp.int32, (BLK, members * BLK), 0)
        query_at = lax.broadcasted_iota(jnp.int32, (BLK, members * BLK), 1) % BLK
        for c in range(kv_heads):
            scores = scores_of(kv_own[0, :, c * HD : (c + 1) * HD], c)
            scores = jnp.where(key_at <= query_at, scores, UNLISTED)
            top = jnp.max(scores, axis=0, keepdims=True)
            expo = jnp.exp(scores - top)
            v_turned = kv_own[1, :, c * HD : (c + 1) * HD].astype(jnp.float32).T.astype(jnp.bfloat16)
            acc_ref[c] = dot(v_turned, expo.astype(jnp.bfloat16))
            max_ref[c] = top
            sum_ref[c] = jnp.sum(expo, axis=0, keepdims=True)

    def earlier_block(slot):
        listed = jnp.max(
            jnp.where(pat_ref[...] == me - 1 - slot, 0.0, UNLISTED), axis=1, keepdims=True
        )
        for c in range(kv_heads):
            scores = scores_of(kv_in[slot, 0, :, c * HD : (c + 1) * HD], c) + listed
            before = max_ref[c]
            top = jnp.maximum(before, jnp.max(scores, axis=0, keepdims=True))
            scale = jnp.exp(before - top)
            expo = jnp.exp(scores - top)
            v_turned = (
                kv_in[slot, 1, :, c * HD : (c + 1) * HD].astype(jnp.float32).T.astype(jnp.bfloat16)
            )
            acc_ref[c] = acc_ref[c] * scale + dot(v_turned, expo.astype(jnp.bfloat16))
            max_ref[c] = top
            sum_ref[c] = sum_ref[c] * scale + jnp.sum(expo, axis=0, keepdims=True)

    ld_copy.wait_recv()
    wide_own = dot(total.T, head_of, EXACT)
    wide_other = dot(jnp.sum(ld_in[...], axis=1, keepdims=True).T, head_of, EXACT)
    decay_other = jnp.exp(wide_other)
    decay_late = jnp.exp(jnp.where(side == 0, wide_other, wide_own))
    decay_pair = jnp.exp(wide_other + wide_own)

    def joined(k):
        own, other = s_own[k].astype(jnp.float32), s_in[k].astype(jnp.float32)
        early, late = jnp.where(side == 0, own, other), jnp.where(side == 0, other, own)
        return decay_late[:, k * 128 : (k + 1) * 128] * early + late

    for k in range(chunks):
        s_copies[k].wait_recv()
        joint = joined(k)

        @pl.when((pair == 0) & has_next)
        def _():
            p_out[k] = joint.astype(state_type)
            p_copies[k].start()

        @pl.when((pair >= 1) & has_next)
        def _():
            joint_ref[k] = joint

    @pl.when(side == 0)
    def _():
        for each in to_pair:
            each.start()

    @pl.when(has_before)
    def _():
        for half in (0, 1):
            to_next[half].wait_recv()

            @pl.when(side == 1)
            def _():
                relay_down[half].start()

    @pl.when(side == 1)
    def _():
        for k in range(chunks):
            at = slice(k * 128, (k + 1) * 128)
            growth = grow_ref[:, at]
            y_ref[:, at] = y_ref[:, at] + dot_state(c_ref[...], s_in[k]) * growth
            grow_ref[:, at] = growth * decay_other[:, at]

    def pass_on(half):
        to_pair[half].wait_recv()

        @pl.when(forwards)
        def _():
            forward[half].start()

    @pl.when(pair >= 2)
    def _():
        own_block()
        earlier_block(1)
        pass_on(0)

    @pl.when(pair >= 3)
    def _():
        pass_on(1)
        earlier_block(0)

    for k in range(chunks):
        at = slice(k * 128, (k + 1) * 128)

        @pl.when(pair >= 1)
        def _():
            p_copies[k].wait_recv()

            @pl.when(has_next)
            def _():
                p_out[k] = (
                    decay_pair[:, at] * p_in[k].astype(jnp.float32) + joint_ref[k]
                ).astype(state_type)
                p_copies[k].start()

        if k == min(1, chunks - 1):
            @pl.when(pair == 2)
            def _():
                pass_on(1)

        y_ref[:, at] = y_ref[:, at] + dot_state(c_ref[...], p_in[k]) * grow_ref[:, at]

    @pl.when(pair < 2)
    def _():
        own_block()

        @pl.when(me >= 1)
        def _():
            pass_on(0)
            pass_on(1)

    gated = y_ref[...]
    square = jnp.sum(gated * gated, axis=1, keepdims=True)
    inverse = lax.rsqrt(square / width + 1e-05)
    ssm_ref[...] = (gated * inverse * gain_ref[...]).astype(jnp.bfloat16)

    @pl.when(pair == 1)
    def _():
        earlier_block(1)

    @pl.when((pair < 3) & (me >= 1))
    def _():
        earlier_block(0)

    @pl.when(me >= 3)
    def _():
        for each in forward:
            each.wait_recv()
        earlier_block(2)

    ld_copy.wait_send()
    for each in s_copies:
        each.wait_send()

    @pl.when(has_next)
    def _():
        for each in to_next + p_copies:
            each.wait_send()

    @pl.when(side == 0)
    def _():
        for each in to_pair:
            each.wait_send()

    @pl.when(has_before & (side == 1))
    def _():
        for each in relay_down:
            each.wait_send()

    @pl.when(forwards)
    def _():
        for each in forward:
            each.wait_send()


def finish(acc_ref, sum_ref, ssm_ref, attn_hbm, ssm_hbm, attn_ref, sems):
    kv_heads, _, rows = acc_ref.shape
    ssm_copy = pltpu.make_async_copy(ssm_ref, ssm_hbm, sems.at[kv_heads])
    ssm_copy.start()
    copies = []
    for c in range(kv_heads):
        mixed = acc_ref[c] / sum_ref[c]
        for j in range(rows // BLK):
            head = c * (rows // BLK) + j
            attn_ref[:, head * HD : (head + 1) * HD] = (
                mixed[:, j * BLK : (j + 1) * BLK].T.astype(jnp.bfloat16)
            )
        at = pl.ds(c * rows, rows)
        copies.append(
            pltpu.make_async_copy(attn_ref.at[:, at], attn_hbm.at[:, at], sems.at[c])
        )
        copies[-1].start()
    for each in copies:
        each.wait()
    ssm_copy.wait()


def on_device(n, queries, keys, values, pattern, x_in, z_gate, bmat, cmat, log_decay, gain):
    state_type = jnp.bfloat16 if n <= 16 else jnp.float32
    heads = log_decay.shape[0]
    width = heads * P_SIZE
    chunks = width // 128
    kv_heads = keys.shape[1] // HD
    rows = queries.shape[1] // keys.shape[1] * BLK
    states = pltpu.VMEM((chunks, N, 128), state_type)
    dma = pltpu.SemaphoreType.DMA
    in_hbm = pl.BlockSpec(memory_space=pltpu.HBM)
    in_vmem = pl.BlockSpec(memory_space=pltpu.VMEM)

    def held(array):
        return pltpu.VMEM(array.shape, array.dtype)

    gain = gain.reshape(1, -1)
    far_inputs = [
        pltpu.with_memory_space_constraint(each, pltpu.HBM)
        for each in (queries, keys, values, pattern, x_in, z_gate, bmat, cmat, log_decay, gain)
    ]
    unscaled, totals, ssm = pl.pallas_call(
        functools.partial(kernel, n, state_type),
        out_shape=(
            jax.ShapeDtypeStruct((kv_heads, HD, rows), jnp.float32),
            jax.ShapeDtypeStruct((kv_heads, 1, rows), jnp.float32),
            jax.ShapeDtypeStruct(x_in.shape, jnp.bfloat16),
        ),
        in_specs=[in_hbm] * 10,
        out_specs=(in_vmem,) * 3,
        scratch_shapes=[
            held(queries), held(pattern), held(x_in), held(z_gate), held(bmat), held(cmat),
            held(log_decay), held(gain),
            pltpu.VMEM((2, BLK, keys.shape[1]), jnp.bfloat16),
            pltpu.VMEM((3, 2, BLK, keys.shape[1]), jnp.bfloat16),
            pltpu.VMEM(log_decay.shape, jnp.float32),
            states, states, states, states,
            pltpu.VMEM((chunks, N, 128), jnp.float32),
            pltpu.VMEM((BLK, width), jnp.float32),
            pltpu.VMEM((BLK, width), jnp.float32),
            pltpu.VMEM((kv_heads, 1, rows), jnp.float32),
            dma((10,)), dma((4, 2)), dma((3, 2)), dma, dma,
            dma((chunks,)), dma((chunks,)), dma((chunks,)), dma((chunks,)),
        ],
        compiler_params=pltpu.CompilerParams(
            collective_id=0, has_side_effects=True, vmem_limit_bytes=32 * 1024 * 1024
        ),
    )(*far_inputs)
    return pl.pallas_call(
        finish,
        out_shape=(
            jax.ShapeDtypeStruct(queries.shape, jnp.bfloat16),
            jax.ShapeDtypeStruct(x_in.shape, jnp.bfloat16),
        ),
        in_specs=[in_vmem] * 3,
        out_specs=(in_hbm, in_hbm),
        scratch_shapes=[held(queries), dma((kv_heads + 1,))],
        compiler_params=pltpu.CompilerParams(vmem_limit_bytes=32 * 1024 * 1024),
    )(unscaled, totals, ssm)


def solution(mesh):
    rows = P(("groups", "ctx"), "head")
    placed = (
        rows, rows, rows, P(("groups", "ctx"), None), rows, rows, rows, rows,
        P(("groups", "head"), "ctx"), P("head"),
    )
    return jax.shard_map(
        functools.partial(on_device, mesh.shape["ctx"]),
        mesh=mesh,
        in_specs=placed,
        out_specs=(rows, rows),
        check_vma=False,
    )
```

```python
import functools

import jax
import jax.numpy as jnp
from jax import lax
from jax.experimental import pallas as pl
from jax.experimental.pallas import tpu as pltpu
from jax.sharding import PartitionSpec as P

BLK = 128
HD = 128
P_SIZE = 64
N = 128
UNLISTED = -1e30
EXACT = lax.Precision.HIGHEST
MESH = pl.DeviceIdType.MESH


def dot(a, b, precision=None):
    return jnp.dot(a, b, preferred_element_type=jnp.float32, precision=precision)


def dot_rows(a, b):
    return lax.dot_general(a, b, (((1,), (1,)), ((), ())), preferred_element_type=jnp.float32)


def dot_state(c, state):
    if state.dtype == jnp.bfloat16:
        return dot(c, state)
    upper = state.astype(jnp.bfloat16)
    lower = (state - upper.astype(jnp.float32)).astype(jnp.bfloat16)
    return dot(c, upper) + dot(c, lower)


def kernel(
    n, state_type,
    q_hbm, k_hbm, v_hbm, pat_hbm, x_hbm, z_hbm, b_hbm, c_hbm, ld_hbm, gain_hbm,
    acc_ref, sum_ref, ssm_ref,
    q_ref, pat_ref, x_ref, z_ref, b_ref, c_ref, ld_ref, gain_ref,
    kv_own, kv_in, ld_in, s_own, s_in, p_out, p_in, y_ref, grow_ref, max_ref,
    load_sem, kv_send, kv_recv, ld_send, ld_recv, s_send, s_recv, p_send, p_recv,
):
    me = lax.axis_index("ctx")
    pair = me // 2
    side = me % 2
    partner = me + 1 - 2 * side
    has_next = me + 2 < n
    has_before = me >= 2
    heads = ld_ref.shape[0]
    width = heads * P_SIZE
    chunks = width // 128
    kv_heads = kv_own.shape[2] // HD
    members = q_ref.shape[1] // kv_own.shape[2]

    barrier = pltpu.get_barrier_semaphore()
    for away in (-2, -1, 1, 2):
        @pl.when((me + away >= 0) & (me + away < n))
        def _():
            pl.semaphore_signal(barrier, inc=1, device_id={"ctx": me + away}, device_id_type=MESH)

    moves = (
        (ld_hbm, ld_ref), (b_hbm, b_ref), (x_hbm, x_ref), (k_hbm, kv_own.at[0]),
        (v_hbm, kv_own.at[1]), (c_hbm, c_ref), (z_hbm, z_ref), (q_hbm, q_ref),
        (gain_hbm, gain_ref), (pat_hbm, pat_ref),
    )
    loads = [pltpu.make_async_copy(src, dst, load_sem.at[i]) for i, (src, dst) in enumerate(moves)]
    for each in loads:
        each.start()
    ld_load, b_load, x_load, k_load, v_load, c_load, z_load, q_load, gain_load, pat_load = loads

    def copy(src, dst, send_sem, recv_sem, target):
        return pltpu.make_async_remote_copy(
            src_ref=src, dst_ref=dst, send_sem=send_sem, recv_sem=recv_sem,
            device_id={"ctx": target}, device_id_type=MESH,
        )

    def kv_copies(src, slot, which, target):
        return [
            copy(
                src.at[half], kv_in.at[slot, half], kv_send.at[which, half],
                kv_recv.at[slot, half], target,
            )
            for half in (0, 1)
        ]

    to_next = kv_copies(kv_own, 1, 0, me + 2)
    to_pair = kv_copies(kv_own, 0, 1, me + 1)
    relay_up = kv_copies(kv_in.at[1], 2, 2, me + 1)
    relay_down = kv_copies(kv_in.at[1], 0, 3, me - 1)
    ld_copy = copy(ld_ref, ld_in, ld_send, ld_recv, partner)
    s_copies = [
        copy(s_own.at[k], s_in.at[k], s_send.at[k], s_recv.at[k], partner) for k in range(chunks)
    ]
    p_copies = [
        copy(p_out.at[k], p_in.at[k], p_send.at[k], p_recv.at[k], me + 2) for k in range(chunks)
    ]

    @pl.when(pair == 0)
    def _():
        p_in[...] = jnp.zeros_like(p_in)

    row = lax.broadcasted_iota(jnp.int32, (BLK, BLK), 0)
    col = lax.broadcasted_iota(jnp.int32, (BLK, BLK), 1)
    head_of = (
        lax.broadcasted_iota(jnp.int32, (heads, width), 1) // P_SIZE
        == lax.broadcasted_iota(jnp.int32, (heads, width), 0)
    ).astype(jnp.float32)

    def per_head_pair(k, matrix_of):
        x_pair = x_ref[:, k * 128 : (k + 1) * 128]
        first = dot(matrix_of(2 * k).astype(jnp.bfloat16), x_pair)
        second = dot(matrix_of(2 * k + 1).astype(jnp.bfloat16), x_pair)
        return jnp.where(col < P_SIZE, first, second)

    ld_load.wait()
    cum_row = dot(ld_ref[...], (row <= col).astype(jnp.float32), EXACT)
    total = cum_row[:, BLK - 1 :]
    fading = jnp.exp(total - cum_row)
    b_load.wait()
    b_turned = b_ref[...].astype(jnp.float32).T
    x_load.wait()
    for k in range(chunks):
        summary = per_head_pair(k, lambda h: b_turned * fading[h : h + 1, :])
        s_own[k] = summary.astype(state_type)

    peers = jnp.minimum(me, 2) + jnp.minimum(n - 1 - me, 2)
    pl.semaphore_wait(barrier, peers)

    ld_copy.start()
    for each in s_copies:
        each.start()
    k_load.wait()
    v_load.wait()

    @pl.when(has_next)
    def _():
        for each in to_next:
            each.start()

    cum_col = cum_row.T
    c_load.wait()
    affinity = dot_rows(c_ref[...], b_ref[...])
    grow = dot(jnp.exp(cum_col), head_of, EXACT)
    z_load.wait()
    for k in range(chunks):
        at = slice(k * 128, (k + 1) * 128)

        def mixing(h):
            spread = cum_col[:, h : h + 1] - cum_row[h : h + 1, :]
            return affinity * jnp.exp(jnp.where(row >= col, spread, -jnp.inf))

        z = z_ref[:, at].astype(jnp.float32)
        gate = z / (1.0 + jnp.exp(-z))
        y_ref[:, at] = per_head_pair(k, mixing) * gate
        grow_ref[:, at] = grow[:, at] * gate
    q_load.wait()
    pat_load.wait()
    gain_load.wait()

    def head_rows(c):
        return jnp.concatenate(
            [q_ref[:, (c * members + j) * HD : (c * members + j + 1) * HD] for j in range(members)],
            axis=0,
        )

    def scores_of(keys, c):
        return dot_rows(keys, head_rows(c)) * HD ** (-0.5)

    def own_block():
        key_at = lax.broadcasted_iota(jnp.int32, (BLK, members * BLK), 0)
        query_at = lax.broadcasted_iota(jnp.int32, (BLK, members * BLK), 1) % BLK
        for c in range(kv_heads):
            scores = scores_of(kv_own[0, :, c * HD : (c + 1) * HD], c)
            scores = jnp.where(key_at <= query_at, scores, UNLISTED)
            top = jnp.max(scores, axis=0, keepdims=True)
            expo = jnp.exp(scores - top)
            v_turned = kv_own[1, :, c * HD : (c + 1) * HD].astype(jnp.float32).T.astype(jnp.bfloat16)
            acc_ref[c] = dot(v_turned, expo.astype(jnp.bfloat16))
            max_ref[c] = top
            sum_ref[c] = jnp.sum(expo, axis=0, keepdims=True)

    def earlier_block(slot):
        listed = jnp.max(
            jnp.where(pat_ref[...] == me - 1 - slot, 0.0, UNLISTED), axis=1, keepdims=True
        )
        for c in range(kv_heads):
            scores = scores_of(kv_in[slot, 0, :, c * HD : (c + 1) * HD], c) + listed
            before = max_ref[c]
            top = jnp.maximum(before, jnp.max(scores, axis=0, keepdims=True))
            scale = jnp.exp(before - top)
            expo = jnp.exp(scores - top)
            v_turned = (
                kv_in[slot, 1, :, c * HD : (c + 1) * HD].astype(jnp.float32).T.astype(jnp.bfloat16)
            )
            acc_ref[c] = acc_ref[c] * scale + dot(v_turned, expo.astype(jnp.bfloat16))
            max_ref[c] = top
            sum_ref[c] = sum_ref[c] * scale + jnp.sum(expo, axis=0, keepdims=True)

    def arrive_and_use(slot):
        if slot != 1:
            for each in kv_copies(kv_own, slot, 0, me):
                each.wait_recv()
        earlier_block(slot)

    ld_copy.wait_recv()
    wide_own = dot(total.T, head_of, EXACT)
    wide_other = dot(jnp.sum(ld_in[...], axis=1, keepdims=True).T, head_of, EXACT)
    decay_other = jnp.exp(wide_other)
    decay_late = jnp.exp(jnp.where(side == 0, wide_other, wide_own))
    decay_pair = jnp.exp(wide_other + wide_own)

    def joined(k):
        own, other = s_own[k].astype(jnp.float32), s_in[k].astype(jnp.float32)
        early, late = jnp.where(side == 0, own, other), jnp.where(side == 0, other, own)
        return decay_late[:, k * 128 : (k + 1) * 128] * early + late

    for k in range(chunks):
        s_copies[k].wait_recv()

        @pl.when((pair == 0) & has_next)
        def _():
            p_out[k] = joined(k).astype(state_type)
            p_copies[k].start()

    @pl.when(side == 0)
    def _():
        for each in to_pair:
            each.start()

    @pl.when(has_before)
    def _():
        for half in (0, 1):
            to_next[half].wait_recv()

            @pl.when((side == 0) | has_next)
            def _():
                relay_up[half].start()

            @pl.when(side == 1)
            def _():
                relay_down[half].start()

    @pl.when(side == 1)
    def _():
        for k in range(chunks):
            at = slice(k * 128, (k + 1) * 128)
            growth = grow_ref[:, at]
            y_ref[:, at] = y_ref[:, at] + dot_state(c_ref[...], s_in[k]) * growth
            grow_ref[:, at] = growth * decay_other[:, at]

    @pl.when(pair >= 2)
    def _():
        own_block()

    @pl.when(pair >= 2)
    def _():
        earlier_block(1)

    @pl.when(pair >= 3)
    def _():
        arrive_and_use(0)
        arrive_and_use(2)

    for k in range(chunks):
        at = slice(k * 128, (k + 1) * 128)

        @pl.when(pair >= 1)
        def _():
            p_copies[k].wait_recv()

            @pl.when(has_next)
            def _():
                p_out[k] = (
                    decay_pair[:, at] * p_in[k].astype(jnp.float32) + joined(k)
                ).astype(state_type)
                p_copies[k].start()

        y_ref[:, at] = y_ref[:, at] + dot_state(c_ref[...], p_in[k]) * grow_ref[:, at]
    gated = y_ref[...]
    square = jnp.sum(gated * gated, axis=1, keepdims=True)
    inverse = lax.rsqrt(square / width + 1e-05)
    ssm_ref[...] = (gated * inverse * gain_ref[...]).astype(jnp.bfloat16)

    @pl.when(pair < 2)
    def _():
        own_block()

    @pl.when(pair == 1)
    def _():
        earlier_block(1)

    @pl.when((pair < 3) & (me >= 1))
    def _():
        arrive_and_use(0)

    @pl.when((pair < 3) & (me >= 3))
    def _():
        arrive_and_use(2)

    ld_copy.wait_send()
    for each in s_copies:
        each.wait_send()

    @pl.when(has_next)
    def _():
        for each in to_next + p_copies:
            each.wait_send()

    @pl.when(side == 0)
    def _():
        for each in to_pair:
            each.wait_send()

    @pl.when(has_before & ((side == 0) | has_next))
    def _():
        for each in relay_up:
            each.wait_send()

    @pl.when(has_before & (side == 1))
    def _():
        for each in relay_down:
            each.wait_send()


def finish(acc_ref, sum_ref, ssm_ref, attn_hbm, ssm_hbm, attn_ref, sems):
    kv_heads, _, rows = acc_ref.shape
    ssm_copy = pltpu.make_async_copy(ssm_ref, ssm_hbm, sems.at[kv_heads])
    ssm_copy.start()
    copies = []
    for c in range(kv_heads):
        mixed = acc_ref[c] / sum_ref[c]
        for j in range(rows // BLK):
            head = c * (rows // BLK) + j
            attn_ref[:, head * HD : (head + 1) * HD] = (
                mixed[:, j * BLK : (j + 1) * BLK].T.astype(jnp.bfloat16)
            )
        at = pl.ds(c * rows, rows)
        copies.append(
            pltpu.make_async_copy(attn_ref.at[:, at], attn_hbm.at[:, at], sems.at[c])
        )
        copies[-1].start()
    for each in copies:
        each.wait()
    ssm_copy.wait()


def on_device(n, queries, keys, values, pattern, x_in, z_gate, bmat, cmat, log_decay, gain):
    state_type = jnp.bfloat16 if n <= 16 else jnp.float32
    heads = log_decay.shape[0]
    width = heads * P_SIZE
    chunks = width // 128
    kv_heads = keys.shape[1] // HD
    rows = queries.shape[1] // keys.shape[1] * BLK
    states = pltpu.VMEM((chunks, N, 128), state_type)
    dma = pltpu.SemaphoreType.DMA
    in_hbm = pl.BlockSpec(memory_space=pltpu.HBM)
    in_vmem = pl.BlockSpec(memory_space=pltpu.VMEM)

    def held(array):
        return pltpu.VMEM(array.shape, array.dtype)

    gain = gain.reshape(1, -1)
    far_inputs = [
        pltpu.with_memory_space_constraint(each, pltpu.HBM)
        for each in (queries, keys, values, pattern, x_in, z_gate, bmat, cmat, log_decay, gain)
    ]
    unscaled, totals, ssm = pl.pallas_call(
        functools.partial(kernel, n, state_type),
        out_shape=(
            jax.ShapeDtypeStruct((kv_heads, HD, rows), jnp.float32),
            jax.ShapeDtypeStruct((kv_heads, 1, rows), jnp.float32),
            jax.ShapeDtypeStruct(x_in.shape, jnp.bfloat16),
        ),
        in_specs=[in_hbm] * 10,
        out_specs=(in_vmem,) * 3,
        scratch_shapes=[
            held(queries), held(pattern), held(x_in), held(z_gate), held(bmat), held(cmat),
            held(log_decay), held(gain),
            pltpu.VMEM((2, BLK, keys.shape[1]), jnp.bfloat16),
            pltpu.VMEM((3, 2, BLK, keys.shape[1]), jnp.bfloat16),
            pltpu.VMEM(log_decay.shape, jnp.float32),
            states, states, states, states,
            pltpu.VMEM((BLK, width), jnp.float32),
            pltpu.VMEM((BLK, width), jnp.float32),
            pltpu.VMEM((kv_heads, 1, rows), jnp.float32),
            dma((10,)), dma((4, 2)), dma((3, 2)), dma, dma,
            dma((chunks,)), dma((chunks,)), dma((chunks,)), dma((chunks,)),
        ],
        compiler_params=pltpu.CompilerParams(
            collective_id=0, has_side_effects=True, vmem_limit_bytes=32 * 1024 * 1024
        ),
    )(*far_inputs)
    return pl.pallas_call(
        finish,
        out_shape=(
            jax.ShapeDtypeStruct(queries.shape, jnp.bfloat16),
            jax.ShapeDtypeStruct(x_in.shape, jnp.bfloat16),
        ),
        in_specs=[in_vmem] * 3,
        out_specs=(in_hbm, in_hbm),
        scratch_shapes=[held(queries), dma((kv_heads + 1,))],
        compiler_params=pltpu.CompilerParams(vmem_limit_bytes=32 * 1024 * 1024),
    )(unscaled, totals, ssm)


def solution(mesh):
    rows = P(("groups", "ctx"), "head")
    placed = (
        rows, rows, rows, P(("groups", "ctx"), None), rows, rows, rows, rows,
        P(("groups", "head"), "ctx"), P("head"),
    )
    return jax.shard_map(
        functools.partial(on_device, mesh.shape["ctx"]),
        mesh=mesh,
        in_specs=placed,
        out_specs=(rows, rows),
        check_vma=False,
    )
```

```python
import functools

import jax
import jax.numpy as jnp
from jax import lax
from jax.experimental import pallas as pl
from jax.experimental.pallas import tpu as pltpu
from jax.sharding import PartitionSpec as P

BLK = 128
HD = 128
P_SIZE = 64
N = 128
UNLISTED = -1e30
EXACT = lax.Precision.HIGHEST
MESH = pl.DeviceIdType.MESH


def dot(a, b, precision=None):
    return jnp.dot(a, b, preferred_element_type=jnp.float32, precision=precision)


def dot_rows(a, b):
    return lax.dot_general(a, b, (((1,), (1,)), ((), ())), preferred_element_type=jnp.float32)


def dot_state(c, state):
    if state.dtype == jnp.bfloat16:
        return dot(c, state)
    upper = state.astype(jnp.bfloat16)
    lower = (state - upper.astype(jnp.float32)).astype(jnp.bfloat16)
    return dot(c, upper) + dot(c, lower)


def kernel(
    n, state_type,
    q_hbm, k_hbm, v_hbm, pat_hbm, x_hbm, z_hbm, b_hbm, c_hbm, ld_hbm, gain_hbm,
    acc_ref, sum_ref, ssm_ref,
    q_ref, pat_ref, x_ref, z_ref, b_ref, c_ref, ld_ref, gain_ref,
    kv_own, kv_in, ld_in, s_own, s_in, p_out, p_in, y_ref, grow_ref, max_ref,
    load_sem, kv_send, kv_recv, ld_send, ld_recv, s_send, s_recv, p_send, p_recv,
):
    me = lax.axis_index("ctx")
    pair = me // 2
    side = me % 2
    partner = me + 1 - 2 * side
    has_next = me + 2 < n
    has_before = me >= 2
    heads = ld_ref.shape[0]
    width = heads * P_SIZE
    chunks = width // 128
    kv_heads = kv_own.shape[2] // HD
    members = q_ref.shape[1] // kv_own.shape[2]

    barrier = pltpu.get_barrier_semaphore()
    for away in (-2, -1, 1, 2):
        @pl.when((me + away >= 0) & (me + away < n))
        def _():
            pl.semaphore_signal(barrier, inc=1, device_id={"ctx": me + away}, device_id_type=MESH)

    moves = (
        (ld_hbm, ld_ref), (b_hbm, b_ref), (x_hbm, x_ref), (k_hbm, kv_own.at[0]),
        (v_hbm, kv_own.at[1]), (c_hbm, c_ref), (z_hbm, z_ref), (q_hbm, q_ref),
        (gain_hbm, gain_ref), (pat_hbm, pat_ref),
    )
    loads = [pltpu.make_async_copy(src, dst, load_sem.at[i]) for i, (src, dst) in enumerate(moves)]
    for each in loads:
        each.start()
    ld_load, b_load, x_load, k_load, v_load, c_load, z_load, q_load, gain_load, pat_load = loads

    def copy(src, dst, send_sem, recv_sem, target):
        return pltpu.make_async_remote_copy(
            src_ref=src, dst_ref=dst, send_sem=send_sem, recv_sem=recv_sem,
            device_id={"ctx": target}, device_id_type=MESH,
        )

    def kv_copies(src, slot, which, target):
        return [
            copy(
                src.at[half], kv_in.at[slot, half], kv_send.at[which, half],
                kv_recv.at[slot, half], target,
            )
            for half in (0, 1)
        ]

    to_next = kv_copies(kv_own, 1, 0, me + 2)
    to_pair = kv_copies(kv_own, 0, 1, me + 1)
    relay_up = kv_copies(kv_in.at[1], 2, 2, me + 1)
    relay_down = kv_copies(kv_in.at[1], 0, 3, me - 1)
    ld_copy = copy(ld_ref, ld_in, ld_send, ld_recv, partner)
    s_copies = [
        copy(s_own.at[k], s_in.at[k], s_send.at[k], s_recv.at[k], partner) for k in range(chunks)
    ]
    p_copies = [
        copy(p_out.at[k], p_in.at[k], p_send.at[k], p_recv.at[k], me + 2) for k in range(chunks)
    ]

    @pl.when(pair == 0)
    def _():
        p_in[...] = jnp.zeros_like(p_in)

    row = lax.broadcasted_iota(jnp.int32, (BLK, BLK), 0)
    col = lax.broadcasted_iota(jnp.int32, (BLK, BLK), 1)
    head_of = (
        lax.broadcasted_iota(jnp.int32, (heads, width), 1) // P_SIZE
        == lax.broadcasted_iota(jnp.int32, (heads, width), 0)
    ).astype(jnp.float32)

    def per_head_pair(k, matrix_of):
        x_pair = x_ref[:, k * 128 : (k + 1) * 128]
        first = dot(matrix_of(2 * k).astype(jnp.bfloat16), x_pair)
        second = dot(matrix_of(2 * k + 1).astype(jnp.bfloat16), x_pair)
        return jnp.where(col < P_SIZE, first, second)

    ld_load.wait()
    cum_row = dot(ld_ref[...], (row <= col).astype(jnp.float32), EXACT)
    total = cum_row[:, BLK - 1 :]
    fading = jnp.exp(total - cum_row)
    b_load.wait()
    b_turned = b_ref[...].astype(jnp.float32).T
    x_load.wait()
    for k in range(chunks):
        summary = per_head_pair(k, lambda h: b_turned * fading[h : h + 1, :])
        s_own[k] = summary.astype(state_type)

    peers = jnp.minimum(me, 2) + jnp.minimum(n - 1 - me, 2)
    pl.semaphore_wait(barrier, peers)

    ld_copy.start()
    for each in s_copies:
        each.start()
    k_load.wait()
    v_load.wait()

    @pl.when(has_next)
    def _():
        for each in to_next:
            each.start()

    cum_col = cum_row.T
    c_load.wait()
    affinity = dot_rows(c_ref[...], b_ref[...])
    grow = dot(jnp.exp(cum_col), head_of, EXACT)
    z_load.wait()
    for k in range(chunks):
        at = slice(k * 128, (k + 1) * 128)

        def mixing(h):
            spread = cum_col[:, h : h + 1] - cum_row[h : h + 1, :]
            return affinity * jnp.exp(jnp.where(row >= col, spread, -jnp.inf))

        z = z_ref[:, at].astype(jnp.float32)
        gate = z / (1.0 + jnp.exp(-z))
        y_ref[:, at] = per_head_pair(k, mixing) * gate
        grow_ref[:, at] = grow[:, at] * gate
    q_load.wait()
    pat_load.wait()
    gain_load.wait()

    def head_rows(c):
        return jnp.concatenate(
            [q_ref[:, (c * members + j) * HD : (c * members + j + 1) * HD] for j in range(members)],
            axis=0,
        )

    def scores_of(keys, c):
        return dot_rows(keys, head_rows(c)) * HD ** (-0.5)

    def own_block():
        key_at = lax.broadcasted_iota(jnp.int32, (BLK, members * BLK), 0)
        query_at = lax.broadcasted_iota(jnp.int32, (BLK, members * BLK), 1) % BLK
        for c in range(kv_heads):
            scores = scores_of(kv_own[0, :, c * HD : (c + 1) * HD], c)
            scores = jnp.where(key_at <= query_at, scores, UNLISTED)
            top = jnp.max(scores, axis=0, keepdims=True)
            expo = jnp.exp(scores - top)
            v_turned = kv_own[1, :, c * HD : (c + 1) * HD].astype(jnp.float32).T.astype(jnp.bfloat16)
            acc_ref[c] = dot(v_turned, expo.astype(jnp.bfloat16))
            max_ref[c] = top
            sum_ref[c] = jnp.sum(expo, axis=0, keepdims=True)

    def earlier_block(slot):
        listed = jnp.max(
            jnp.where(pat_ref[...] == me - 1 - slot, 0.0, UNLISTED), axis=1, keepdims=True
        )
        for c in range(kv_heads):
            scores = scores_of(kv_in[slot, 0, :, c * HD : (c + 1) * HD], c) + listed
            before = max_ref[c]
            top = jnp.maximum(before, jnp.max(scores, axis=0, keepdims=True))
            scale = jnp.exp(before - top)
            expo = jnp.exp(scores - top)
            v_turned = (
                kv_in[slot, 1, :, c * HD : (c + 1) * HD].astype(jnp.float32).T.astype(jnp.bfloat16)
            )
            acc_ref[c] = acc_ref[c] * scale + dot(v_turned, expo.astype(jnp.bfloat16))
            max_ref[c] = top
            sum_ref[c] = sum_ref[c] * scale + jnp.sum(expo, axis=0, keepdims=True)

    def arrive_and_use(slot):
        if slot != 1:
            for each in kv_copies(kv_own, slot, 0, me):
                each.wait_recv()
        earlier_block(slot)

    ld_copy.wait_recv()
    wide_own = dot(total.T, head_of, EXACT)
    wide_other = dot(jnp.sum(ld_in[...], axis=1, keepdims=True).T, head_of, EXACT)
    decay_other = jnp.exp(wide_other)
    decay_late = jnp.exp(jnp.where(side == 0, wide_other, wide_own))
    decay_pair = jnp.exp(wide_other + wide_own)

    def joined(k):
        own, other = s_own[k].astype(jnp.float32), s_in[k].astype(jnp.float32)
        early, late = jnp.where(side == 0, own, other), jnp.where(side == 0, other, own)
        return decay_late[:, k * 128 : (k + 1) * 128] * early + late

    for k in range(chunks):
        s_copies[k].wait_recv()

        @pl.when((pair == 0) & has_next)
        def _():
            p_out[k] = joined(k).astype(state_type)
            p_copies[k].start()

    @pl.when(side == 0)
    def _():
        for each in to_pair:
            each.start()

    @pl.when(has_before)
    def _():
        for half in (0, 1):
            to_next[half].wait_recv()

            @pl.when((side == 0) | has_next)
            def _():
                relay_up[half].start()

            @pl.when(side == 1)
            def _():
                relay_down[half].start()

    @pl.when(side == 1)
    def _():
        for k in range(chunks):
            at = slice(k * 128, (k + 1) * 128)
            growth = grow_ref[:, at]
            y_ref[:, at] = y_ref[:, at] + dot_state(c_ref[...], s_in[k]) * growth
            grow_ref[:, at] = growth * decay_other[:, at]

    @pl.when(pair >= 2)
    def _():
        own_block()

    @pl.when(pair >= 2)
    def _():
        earlier_block(1)

    @pl.when(pair >= 3)
    def _():
        arrive_and_use(0)

    for k in range(chunks):
        at = slice(k * 128, (k + 1) * 128)

        @pl.when(pair >= 1)
        def _():
            p_copies[k].wait_recv()

            @pl.when(has_next)
            def _():
                p_out[k] = (
                    decay_pair[:, at] * p_in[k].astype(jnp.float32) + joined(k)
                ).astype(state_type)
                p_copies[k].start()

        y_ref[:, at] = y_ref[:, at] + dot_state(c_ref[...], p_in[k]) * grow_ref[:, at]
    gated = y_ref[...]
    square = jnp.sum(gated * gated, axis=1, keepdims=True)
    inverse = lax.rsqrt(square / width + 1e-05)
    ssm_ref[...] = (gated * inverse * gain_ref[...]).astype(jnp.bfloat16)

    @pl.when(pair < 2)
    def _():
        own_block()

    @pl.when(pair == 1)
    def _():
        earlier_block(1)

    @pl.when((pair < 3) & (me >= 1))
    def _():
        arrive_and_use(0)

    @pl.when(me >= 3)
    def _():
        arrive_and_use(2)

    ld_copy.wait_send()
    for each in s_copies:
        each.wait_send()

    @pl.when(has_next)
    def _():
        for each in to_next + p_copies:
            each.wait_send()

    @pl.when(side == 0)
    def _():
        for each in to_pair:
            each.wait_send()

    @pl.when(has_before & ((side == 0) | has_next))
    def _():
        for each in relay_up:
            each.wait_send()

    @pl.when(has_before & (side == 1))
    def _():
        for each in relay_down:
            each.wait_send()


def finish(acc_ref, sum_ref, ssm_ref, attn_hbm, ssm_hbm, attn_ref, sems):
    kv_heads, _, rows = acc_ref.shape
    ssm_copy = pltpu.make_async_copy(ssm_ref, ssm_hbm, sems.at[kv_heads])
    ssm_copy.start()
    copies = []
    for c in range(kv_heads):
        mixed = acc_ref[c] / sum_ref[c]
        for j in range(rows // BLK):
            head = c * (rows // BLK) + j
            attn_ref[:, head * HD : (head + 1) * HD] = (
                mixed[:, j * BLK : (j + 1) * BLK].T.astype(jnp.bfloat16)
            )
        at = pl.ds(c * rows, rows)
        copies.append(
            pltpu.make_async_copy(attn_ref.at[:, at], attn_hbm.at[:, at], sems.at[c])
        )
        copies[-1].start()
    for each in copies:
        each.wait()
    ssm_copy.wait()


def on_device(n, queries, keys, values, pattern, x_in, z_gate, bmat, cmat, log_decay, gain):
    state_type = jnp.bfloat16 if n <= 16 else jnp.float32
    heads = log_decay.shape[0]
    width = heads * P_SIZE
    chunks = width // 128
    kv_heads = keys.shape[1] // HD
    rows = queries.shape[1] // keys.shape[1] * BLK
    states = pltpu.VMEM((chunks, N, 128), state_type)
    dma = pltpu.SemaphoreType.DMA
    in_hbm = pl.BlockSpec(memory_space=pltpu.HBM)
    in_vmem = pl.BlockSpec(memory_space=pltpu.VMEM)

    def held(array):
        return pltpu.VMEM(array.shape, array.dtype)

    gain = gain.reshape(1, -1)
    far_inputs = [
        pltpu.with_memory_space_constraint(each, pltpu.HBM)
        for each in (queries, keys, values, pattern, x_in, z_gate, bmat, cmat, log_decay, gain)
    ]
    unscaled, totals, ssm = pl.pallas_call(
        functools.partial(kernel, n, state_type),
        out_shape=(
            jax.ShapeDtypeStruct((kv_heads, HD, rows), jnp.float32),
            jax.ShapeDtypeStruct((kv_heads, 1, rows), jnp.float32),
            jax.ShapeDtypeStruct(x_in.shape, jnp.bfloat16),
        ),
        in_specs=[in_hbm] * 10,
        out_specs=(in_vmem,) * 3,
        scratch_shapes=[
            held(queries), held(pattern), held(x_in), held(z_gate), held(bmat), held(cmat),
            held(log_decay), held(gain),
            pltpu.VMEM((2, BLK, keys.shape[1]), jnp.bfloat16),
            pltpu.VMEM((3, 2, BLK, keys.shape[1]), jnp.bfloat16),
            pltpu.VMEM(log_decay.shape, jnp.float32),
            states, states, states, states,
            pltpu.VMEM((BLK, width), jnp.float32),
            pltpu.VMEM((BLK, width), jnp.float32),
            pltpu.VMEM((kv_heads, 1, rows), jnp.float32),
            dma((10,)), dma((4, 2)), dma((3, 2)), dma, dma,
            dma((chunks,)), dma((chunks,)), dma((chunks,)), dma((chunks,)),
        ],
        compiler_params=pltpu.CompilerParams(
            collective_id=0, has_side_effects=True, vmem_limit_bytes=32 * 1024 * 1024
        ),
    )(*far_inputs)
    return pl.pallas_call(
        finish,
        out_shape=(
            jax.ShapeDtypeStruct(queries.shape, jnp.bfloat16),
            jax.ShapeDtypeStruct(x_in.shape, jnp.bfloat16),
        ),
        in_specs=[in_vmem] * 3,
        out_specs=(in_hbm, in_hbm),
        scratch_shapes=[held(queries), dma((kv_heads + 1,))],
        compiler_params=pltpu.CompilerParams(vmem_limit_bytes=32 * 1024 * 1024),
    )(unscaled, totals, ssm)


def solution(mesh):
    rows = P(("groups", "ctx"), "head")
    placed = (
        rows, rows, rows, P(("groups", "ctx"), None), rows, rows, rows, rows,
        P(("groups", "head"), "ctx"), P("head"),
    )
    return jax.shard_map(
        functools.partial(on_device, mesh.shape["ctx"]),
        mesh=mesh,
        in_specs=placed,
        out_specs=(rows, rows),
        check_vma=False,
    )
```

```python
import functools

import jax
import jax.numpy as jnp
from jax import lax
from jax.experimental import pallas as pl
from jax.experimental.pallas import tpu as pltpu
from jax.sharding import PartitionSpec as P

BLK = 128
HD = 128
P_SIZE = 64
N = 128
UNLISTED = -1e30
EXACT = lax.Precision.HIGHEST
MESH = pl.DeviceIdType.MESH


def dot(a, b, precision=None):
    return jnp.dot(a, b, preferred_element_type=jnp.float32, precision=precision)


def dot_rows(a, b):
    return lax.dot_general(a, b, (((1,), (1,)), ((), ())), preferred_element_type=jnp.float32)


def dot_state(c, state):
    if state.dtype == jnp.bfloat16:
        return dot(c, state)
    upper = state.astype(jnp.bfloat16)
    lower = (state - upper.astype(jnp.float32)).astype(jnp.bfloat16)
    return dot(c, upper) + dot(c, lower)


def kernel(
    n, state_type,
    q_hbm, k_hbm, v_hbm, pat_hbm, x_hbm, z_hbm, b_hbm, c_hbm, ld_hbm, gain_hbm,
    acc_ref, sum_ref, ssm_ref,
    q_ref, pat_ref, x_ref, z_ref, b_ref, c_ref, ld_ref, gain_ref,
    kv_own, kv_in, ld_in, s_own, s_in, p_out, p_in, y_ref, grow_ref, max_ref,
    load_sem, kv_send, kv_recv, ld_send, ld_recv, s_send, s_recv, p_send, p_recv,
):
    me = lax.axis_index("ctx")
    pair = me // 2
    side = me % 2
    partner = me + 1 - 2 * side
    has_next = me + 2 < n
    has_before = me >= 2
    heads = ld_ref.shape[0]
    width = heads * P_SIZE
    chunks = width // 128
    kv_heads = kv_own.shape[2] // HD
    members = q_ref.shape[1] // kv_own.shape[2]

    barrier = pltpu.get_barrier_semaphore()
    for away in (-2, -1, 1, 2):
        @pl.when((me + away >= 0) & (me + away < n))
        def _():
            pl.semaphore_signal(barrier, inc=1, device_id={"ctx": me + away}, device_id_type=MESH)

    moves = (
        (ld_hbm, ld_ref), (b_hbm, b_ref), (x_hbm, x_ref), (k_hbm, kv_own.at[0]),
        (v_hbm, kv_own.at[1]), (c_hbm, c_ref), (z_hbm, z_ref), (q_hbm, q_ref),
        (gain_hbm, gain_ref), (pat_hbm, pat_ref),
    )
    loads = [pltpu.make_async_copy(src, dst, load_sem.at[i]) for i, (src, dst) in enumerate(moves)]
    for each in loads:
        each.start()
    ld_load, b_load, x_load, k_load, v_load, c_load, z_load, q_load, gain_load, pat_load = loads

    def copy(src, dst, send_sem, recv_sem, target):
        return pltpu.make_async_remote_copy(
            src_ref=src, dst_ref=dst, send_sem=send_sem, recv_sem=recv_sem,
            device_id={"ctx": target}, device_id_type=MESH,
        )

    def kv_copies(src, slot, which, target):
        return [
            copy(
                src.at[half], kv_in.at[slot, half], kv_send.at[which, half],
                kv_recv.at[slot, half], target,
            )
            for half in (0, 1)
        ]

    to_next = kv_copies(kv_own, 1, 0, me + 2)
    to_pair = kv_copies(kv_own, 0, 1, me + 1)
    relay_up = kv_copies(kv_in.at[1], 2, 2, me + 1)
    relay_down = kv_copies(kv_in.at[1], 0, 3, me - 1)
    ld_copy = copy(ld_ref, ld_in, ld_send, ld_recv, partner)
    s_copies = [
        copy(s_own.at[k], s_in.at[k], s_send.at[k], s_recv.at[k], partner) for k in range(chunks)
    ]
    p_copies = [
        copy(p_out.at[k], p_in.at[k], p_send.at[k], p_recv.at[k], me + 2) for k in range(chunks)
    ]

    @pl.when(pair == 0)
    def _():
        p_in[...] = jnp.zeros_like(p_in)

    row = lax.broadcasted_iota(jnp.int32, (BLK, BLK), 0)
    col = lax.broadcasted_iota(jnp.int32, (BLK, BLK), 1)
    head_of = (
        lax.broadcasted_iota(jnp.int32, (heads, width), 1) // P_SIZE
        == lax.broadcasted_iota(jnp.int32, (heads, width), 0)
    ).astype(jnp.float32)

    def per_head_pair(k, matrix_of):
        x_pair = x_ref[:, k * 128 : (k + 1) * 128]
        first = dot(matrix_of(2 * k).astype(jnp.bfloat16), x_pair)
        second = dot(matrix_of(2 * k + 1).astype(jnp.bfloat16), x_pair)
        return jnp.where(col < P_SIZE, first, second)

    ld_load.wait()
    cum_row = dot(ld_ref[...], (row <= col).astype(jnp.float32), EXACT)
    total = cum_row[:, BLK - 1 :]
    fading = jnp.exp(total - cum_row)
    b_load.wait()
    b_turned = b_ref[...].astype(jnp.float32).T
    x_load.wait()
    for k in range(chunks):
        summary = per_head_pair(k, lambda h: b_turned * fading[h : h + 1, :])
        s_own[k] = summary.astype(state_type)

    peers = jnp.minimum(me, 2) + jnp.minimum(n - 1 - me, 2)
    pl.semaphore_wait(barrier, peers)

    ld_copy.start()
    for each in s_copies:
        each.start()
    k_load.wait()
    v_load.wait()

    @pl.when(has_next)
    def _():
        for each in to_next:
            each.start()

    cum_col = cum_row.T
    c_load.wait()
    affinity = dot_rows(c_ref[...], b_ref[...])
    grow = dot(jnp.exp(cum_col), head_of, EXACT)
    z_load.wait()
    for k in range(chunks):
        at = slice(k * 128, (k + 1) * 128)

        def mixing(h):
            spread = cum_col[:, h : h + 1] - cum_row[h : h + 1, :]
            return affinity * jnp.exp(jnp.where(row >= col, spread, -jnp.inf))

        z = z_ref[:, at].astype(jnp.float32)
        gate = z / (1.0 + jnp.exp(-z))
        y_ref[:, at] = per_head_pair(k, mixing) * gate
        grow_ref[:, at] = grow[:, at] * gate
    q_load.wait()
    pat_load.wait()
    gain_load.wait()

    def head_rows(c):
        return jnp.concatenate(
            [q_ref[:, (c * members + j) * HD : (c * members + j + 1) * HD] for j in range(members)],
            axis=0,
        )

    def scores_of(keys, c):
        return dot_rows(keys, head_rows(c)) * HD ** (-0.5)

    def own_block():
        key_at = lax.broadcasted_iota(jnp.int32, (BLK, members * BLK), 0)
        query_at = lax.broadcasted_iota(jnp.int32, (BLK, members * BLK), 1) % BLK
        for c in range(kv_heads):
            scores = scores_of(kv_own[0, :, c * HD : (c + 1) * HD], c)
            scores = jnp.where(key_at <= query_at, scores, UNLISTED)
            top = jnp.max(scores, axis=0, keepdims=True)
            expo = jnp.exp(scores - top)
            v_turned = kv_own[1, :, c * HD : (c + 1) * HD].astype(jnp.float32).T.astype(jnp.bfloat16)
            acc_ref[c] = dot(v_turned, expo.astype(jnp.bfloat16))
            max_ref[c] = top
            sum_ref[c] = jnp.sum(expo, axis=0, keepdims=True)

    def earlier_block(slot):
        listed = jnp.max(
            jnp.where(pat_ref[...] == me - 1 - slot, 0.0, UNLISTED), axis=1, keepdims=True
        )
        for c in range(kv_heads):
            scores = scores_of(kv_in[slot, 0, :, c * HD : (c + 1) * HD], c) + listed
            before = max_ref[c]
            top = jnp.maximum(before, jnp.max(scores, axis=0, keepdims=True))
            scale = jnp.exp(before - top)
            expo = jnp.exp(scores - top)
            v_turned = (
                kv_in[slot, 1, :, c * HD : (c + 1) * HD].astype(jnp.float32).T.astype(jnp.bfloat16)
            )
            acc_ref[c] = acc_ref[c] * scale + dot(v_turned, expo.astype(jnp.bfloat16))
            max_ref[c] = top
            sum_ref[c] = sum_ref[c] * scale + jnp.sum(expo, axis=0, keepdims=True)

    def arrive_and_use(slot):
        if slot != 1:
            for each in kv_copies(kv_own, slot, 0, me):
                each.wait_recv()
        earlier_block(slot)

    ld_copy.wait_recv()
    wide_own = dot(total.T, head_of, EXACT)
    wide_other = dot(jnp.sum(ld_in[...], axis=1, keepdims=True).T, head_of, EXACT)
    decay_other = jnp.exp(wide_other)
    decay_late = jnp.exp(jnp.where(side == 0, wide_other, wide_own))
    decay_pair = jnp.exp(wide_other + wide_own)

    def joined(k):
        own, other = s_own[k].astype(jnp.float32), s_in[k].astype(jnp.float32)
        early, late = jnp.where(side == 0, own, other), jnp.where(side == 0, other, own)
        return decay_late[:, k * 128 : (k + 1) * 128] * early + late

    for k in range(chunks):
        s_copies[k].wait_recv()

        @pl.when((pair == 0) & has_next)
        def _():
            p_out[k] = joined(k).astype(state_type)
            p_copies[k].start()

    @pl.when(side == 0)
    def _():
        for each in to_pair:
            each.start()

    @pl.when(has_before)
    def _():
        for half in (0, 1):
            to_next[half].wait_recv()

            @pl.when((side == 0) | has_next)
            def _():
                relay_up[half].start()

            @pl.when(side == 1)
            def _():
                relay_down[half].start()

    @pl.when(side == 1)
    def _():
        for k in range(chunks):
            at = slice(k * 128, (k + 1) * 128)
            growth = grow_ref[:, at]
            y_ref[:, at] = y_ref[:, at] + dot_state(c_ref[...], s_in[k]) * growth
            grow_ref[:, at] = growth * decay_other[:, at]

    @pl.when(pair >= 3)
    def _():
        own_block()

    @pl.when(pair >= 3)
    def _():
        earlier_block(1)

    @pl.when(pair >= 3)
    def _():
        arrive_and_use(0)
        arrive_and_use(2)

    for k in range(chunks):
        at = slice(k * 128, (k + 1) * 128)

        @pl.when(pair >= 1)
        def _():
            p_copies[k].wait_recv()

            @pl.when(has_next)
            def _():
                p_out[k] = (
                    decay_pair[:, at] * p_in[k].astype(jnp.float32) + joined(k)
                ).astype(state_type)
                p_copies[k].start()

        y_ref[:, at] = y_ref[:, at] + dot_state(c_ref[...], p_in[k]) * grow_ref[:, at]
    gated = y_ref[...]
    square = jnp.sum(gated * gated, axis=1, keepdims=True)
    inverse = lax.rsqrt(square / width + 1e-05)
    ssm_ref[...] = (gated * inverse * gain_ref[...]).astype(jnp.bfloat16)

    @pl.when(pair < 3)
    def _():
        own_block()

    @pl.when((pair == 1) | (pair == 2))
    def _():
        earlier_block(1)

    @pl.when((pair < 3) & (me >= 1))
    def _():
        arrive_and_use(0)

    @pl.when((pair < 3) & (me >= 3))
    def _():
        arrive_and_use(2)

    ld_copy.wait_send()
    for each in s_copies:
        each.wait_send()

    @pl.when(has_next)
    def _():
        for each in to_next + p_copies:
            each.wait_send()

    @pl.when(side == 0)
    def _():
        for each in to_pair:
            each.wait_send()

    @pl.when(has_before & ((side == 0) | has_next))
    def _():
        for each in relay_up:
            each.wait_send()

    @pl.when(has_before & (side == 1))
    def _():
        for each in relay_down:
            each.wait_send()


def finish(acc_ref, sum_ref, ssm_ref, attn_hbm, ssm_hbm, attn_ref, sems):
    kv_heads, _, rows = acc_ref.shape
    ssm_copy = pltpu.make_async_copy(ssm_ref, ssm_hbm, sems.at[kv_heads])
    ssm_copy.start()
    copies = []
    for c in range(kv_heads):
        mixed = acc_ref[c] / sum_ref[c]
        for j in range(rows // BLK):
            head = c * (rows // BLK) + j
            attn_ref[:, head * HD : (head + 1) * HD] = (
                mixed[:, j * BLK : (j + 1) * BLK].T.astype(jnp.bfloat16)
            )
        at = pl.ds(c * rows, rows)
        copies.append(
            pltpu.make_async_copy(attn_ref.at[:, at], attn_hbm.at[:, at], sems.at[c])
        )
        copies[-1].start()
    for each in copies:
        each.wait()
    ssm_copy.wait()


def on_device(n, queries, keys, values, pattern, x_in, z_gate, bmat, cmat, log_decay, gain):
    state_type = jnp.bfloat16 if n <= 16 else jnp.float32
    heads = log_decay.shape[0]
    width = heads * P_SIZE
    chunks = width // 128
    kv_heads = keys.shape[1] // HD
    rows = queries.shape[1] // keys.shape[1] * BLK
    states = pltpu.VMEM((chunks, N, 128), state_type)
    dma = pltpu.SemaphoreType.DMA
    in_hbm = pl.BlockSpec(memory_space=pltpu.HBM)
    in_vmem = pl.BlockSpec(memory_space=pltpu.VMEM)

    def held(array):
        return pltpu.VMEM(array.shape, array.dtype)

    gain = gain.reshape(1, -1)
    far_inputs = [
        pltpu.with_memory_space_constraint(each, pltpu.HBM)
        for each in (queries, keys, values, pattern, x_in, z_gate, bmat, cmat, log_decay, gain)
    ]
    unscaled, totals, ssm = pl.pallas_call(
        functools.partial(kernel, n, state_type),
        out_shape=(
            jax.ShapeDtypeStruct((kv_heads, HD, rows), jnp.float32),
            jax.ShapeDtypeStruct((kv_heads, 1, rows), jnp.float32),
            jax.ShapeDtypeStruct(x_in.shape, jnp.bfloat16),
        ),
        in_specs=[in_hbm] * 10,
        out_specs=(in_vmem,) * 3,
        scratch_shapes=[
            held(queries), held(pattern), held(x_in), held(z_gate), held(bmat), held(cmat),
            held(log_decay), held(gain),
            pltpu.VMEM((2, BLK, keys.shape[1]), jnp.bfloat16),
            pltpu.VMEM((3, 2, BLK, keys.shape[1]), jnp.bfloat16),
            pltpu.VMEM(log_decay.shape, jnp.float32),
            states, states, states, states,
            pltpu.VMEM((BLK, width), jnp.float32),
            pltpu.VMEM((BLK, width), jnp.float32),
            pltpu.VMEM((kv_heads, 1, rows), jnp.float32),
            dma((10,)), dma((4, 2)), dma((3, 2)), dma, dma,
            dma((chunks,)), dma((chunks,)), dma((chunks,)), dma((chunks,)),
        ],
        compiler_params=pltpu.CompilerParams(
            collective_id=0, has_side_effects=True, vmem_limit_bytes=32 * 1024 * 1024
        ),
    )(*far_inputs)
    return pl.pallas_call(
        finish,
        out_shape=(
            jax.ShapeDtypeStruct(queries.shape, jnp.bfloat16),
            jax.ShapeDtypeStruct(x_in.shape, jnp.bfloat16),
        ),
        in_specs=[in_vmem] * 3,
        out_specs=(in_hbm, in_hbm),
        scratch_shapes=[held(queries), dma((kv_heads + 1,))],
        compiler_params=pltpu.CompilerParams(vmem_limit_bytes=32 * 1024 * 1024),
    )(unscaled, totals, ssm)


def solution(mesh):
    rows = P(("groups", "ctx"), "head")
    placed = (
        rows, rows, rows, P(("groups", "ctx"), None), rows, rows, rows, rows,
        P(("groups", "head"), "ctx"), P("head"),
    )
    return jax.shard_map(
        functools.partial(on_device, mesh.shape["ctx"]),
        mesh=mesh,
        in_specs=placed,
        out_specs=(rows, rows),
        check_vma=False,
    )
```
